512 devices in a mesh: sec: 64 (over y, z), rad: 8 (over x, core).
Axes of the slice: x: 4, y: 4, z: 16, core: 2. Of those that a mesh axis runs over, the one named last changes fastest.
Arguments:
- transmembrane_potential: float32 [65536, 256], P(('sec', 'rad')), may hold values from -0.8 to -0.3
- channel_openness: float32 [3, 65536, 256], P(None, ('sec', 'rad')), may hold values from 0.02 to 0.95
- longitudinal_conductance: float32 [65536], P(('sec', 'rad')), may hold values from 0.05 to 0.4
- sector_map: int32 [65536, 1], P(('sec', 'rad')), may hold values from 0 to 63; in each aligned block of 128 rows (0 to 127, 128 to 255, ...) at most 4 rows name the same one
- cell_index: int32 [65536], P(('sec', 'rad')), may hold values from 0 to 255
- innervating_neuron: int32 [65536], P(('sec', 'rad')), may hold values from 0 to 511
- activation_moment: int32 [512], replicated, may hold values from 0 to 19
- synapse_position: int32 [65536], P(('sec', 'rad')), may hold values from 64 to 191
- radial_basis_matrix: float32 [256, 256], replicated, may hold values from -0.375 to 0.375
- spectrum: float32 [256, 512], P('sec'), may hold values from 1 to 20
Outputs:
- transmembrane_potential_later: float32 [65536, 256], P(('sec', 'rad'))
- channel_openness_later: float32 [3, 65536, 256], P(None, ('sec', 'rad'))
- potential: float32 [256, 256, 2, 512], P('sec', 'rad')
The draws below stay inside these ranges and needn't reach their ends.
Inputs may be any that keep to these rules, and one draw needn't show every extreme that they name: `sector_map`: among the 128 fibres of one device, at most 4 lie in any one sector.
All inputs are finite; a program needn't handle non-finite values.
Results may differ from the reference program's by a relative error of at most 0.00007.
Values sent between devices are 32-bit elements; how exact they have to be, the bound alone decides.
A program may use at most 64 MiB of HBM per device.

```python
import math
import jax
import jax.numpy as jnp
import numpy as np
from jax import lax

AZ = 512
RAD = 256
AXIAL = 256
FIB_DEV = 128
MUS = 512
SUBSTEPS = 10
CAP = 4
CELLS = 256
FIBRES = 65536
N_SEC = 64
N_RAD = 8


def touch_ends(array, own_key, least, high):
    index_at = [jax.random.randint(jax.random.fold_in(own_key, axis), (), 0, length) for axis, length in enumerate(array.shape)]
    widest = array.shape.index(max(array.shape))
    next_to = index_at[:widest] + [(index_at[widest] + 1) % array.shape[widest]] + index_at[widest + 1:]
    return array.at[tuple(index_at)].set(least).at[tuple(next_to)].set(high)


def level_of(key, shape, shards, low, largest):
    loudness, own = 1.0, jax.random.fold_in(key, 6)
    for axis_at, parts in shards:
        heights = jnp.exp(jax.random.uniform(jax.random.fold_in(own, axis_at), (parts,), jnp.float32, low / len(shards), largest / len(shards)))
        loudness = loudness * jnp.repeat(heights, shape[axis_at] // parts).reshape([-1 if axis == axis_at else 1 for axis in range(len(shape))])
    return loudness


def rank_bounds(count, skew):
    weights = [(1 << 20) // math.isqrt(standing ** skew) + 1 for standing in range(1, count + 1)]
    scale = 1 + sum(weights) // (1 << 30)
    return np.cumsum(np.array([max(1, weight // scale) for weight in weights]))


def ranked(stream_key, shape, count, slope):
    grid = rank_bounds(count, slope)
    lot = jax.random.randint(jax.random.fold_in(stream_key, 1), shape, 0, int(grid[count - 1]))
    standing = jnp.searchsorted(jnp.asarray(grid, jnp.int32), lot, side="right")
    return jax.random.permutation(jax.random.fold_in(stream_key, 2), count)[standing].astype(jnp.int32)


def shared_out(own_key, own, number, rows, amount, top, most, lean):
    sequence = jax.random.permutation(own_key, amount)
    crowded, usual = portions_of(amount, rows * top, most, lean, True), portions_of(amount, rows * top, most, lean, False)
    places = jnp.arange(amount)

    def named(lengths, rotation):
        used = int((lengths > 0).sum())
        fixed = max(1, used // 4)
        passed = fixed + (places - fixed + rotation * (used - fixed)) % max(1, amount - fixed)
        return jnp.zeros((amount,), jnp.int32).at[sequence[jnp.where(places < fixed, places, passed)]].set(jnp.asarray(lengths, jnp.int32))

    lengths = jnp.where(number % 4 == 0, named(crowded, number // 4), named(usual, number - number // 4 - 1))
    mixed = jax.random.permutation(jax.random.fold_in(own, 3), amount)
    donor, sink = mixed[0:amount // 2 * 2:2], mixed[1:amount // 2 * 2:2]
    room = jnp.minimum(lengths[donor] - 1, most - lengths[sink]) // 2
    room = jnp.where((donor == sequence[0]) | (sink == sequence[0]) | (lengths[sink] == 0), 0, jnp.maximum(room, 0))
    passed = jax.random.randint(jax.random.fold_in(own, 4), (amount // 2,), 0, 1 << 20) % (room + 1)
    lengths = lengths.at[donor].add(-passed).at[sink].add(passed)
    items = jnp.searchsorted(jnp.cumsum(lengths), jnp.arange(rows * top), side="right").astype(jnp.int32)
    table = items.reshape(top, rows).T
    table = table[jax.random.permutation(jax.random.fold_in(own, 1), rows)]
    rotation = jax.random.randint(jax.random.fold_in(own, 2), (rows, 1), 0, top)
    return jnp.take_along_axis(table, (jnp.arange(top)[None, :] + rotation) % top, axis=1)


def portions_of(count, total, limit, lean, full):
    portions = [(1 << 20) // math.isqrt(grade ** lean) + 1 for grade in range(1, count + 1)]
    largest = limit if full else min(limit, max(-(-total // count), total * portions[0] // sum(portions)))
    least = 1 if total - largest >= count - 1 else 0
    given, surplus = [largest] + [least] * (count - 1), total - largest - least * (count - 1)
    while surplus > 0:
        free = [i for i in range(1, count) if given[i] < largest] or [i for i in range(1, count) if given[i] < limit]
        mass, remaining = sum([portions[i] for i in free]), surplus
        for i in free:
            addition = min(limit - given[i], max(1, remaining * portions[i] // mass), surplus)
            given[i] = given[i] + addition
            surplus = surplus - addition
    return np.array(given)


def gaussian(key, shape, deviation, limit, held_as=jnp.bfloat16):
    return jnp.clip(deviation * jax.random.normal(key, shape, jnp.float32), -limit, limit).astype(held_as)


def setup_inputs(seed: int = 0) -> dict:
    splits = jax.random.split(jax.random.key(seed), 11)
    transmembrane_potential = jnp.clip(-0.8 + 0.5 * jax.random.uniform(splits[0], (FIBRES, AXIAL), jnp.float32) ** level_of(splits[0], (FIBRES, AXIAL), ((0, 512),), -0.2, 0.2), -0.8, -0.3)
    channel_openness = jnp.clip(0.02 + 0.93 * jax.random.uniform(splits[1], (3, FIBRES, AXIAL), jnp.float32) ** level_of(splits[1], (3, FIBRES, AXIAL), ((1, 512),), -0.2, 0.2), 0.02, 0.95)
    longitudinal_conductance = jnp.clip(jnp.exp(math.log(0.4) - 2.0794415 * jax.random.uniform(splits[2], (FIBRES,), jnp.float32) ** level_of(splits[2], (FIBRES,), ((0, 512),), -0.2, 0.2)), 0.05, 0.4)
    sector_map_keys = jax.random.split(jax.random.fold_in(splits[3], 1), FIBRES // FIB_DEV)
    sector_map_turns = jax.random.permutation(jax.random.fold_in(splits[3], 3), FIBRES // FIB_DEV)
    sector_map = jax.vmap(lambda own, number: shared_out(jax.random.fold_in(splits[3], 2), own, number, FIB_DEV, N_SEC, 1, CAP, 2))(sector_map_keys, sector_map_turns).reshape((FIBRES, 1))
    cell_index = touch_ends(jax.random.randint(splits[4], (FIBRES,), 0, CELLS), jax.random.fold_in(splits[4], 1), 0, CELLS - 1).astype(jnp.int32)
    innervating_neuron = touch_ends(ranked(splits[5], (FIBRES,), MUS, 2), jax.random.fold_in(splits[5], 3), 0, MUS - 1).astype(jnp.int32)
    activation_moment = touch_ends(jax.random.randint(splits[6], (MUS,), 0, 2 * SUBSTEPS), jax.random.fold_in(splits[6], 1), 0, (2 * SUBSTEPS) - 1).astype(jnp.int32)
    synapse_position = touch_ends(jax.random.randint(splits[7], (FIBRES,), AXIAL // 4, 3 * AXIAL // 4), jax.random.fold_in(splits[7], 1), AXIAL // 4, (3 * AXIAL // 4) - 1).astype(jnp.int32)
    radial_basis_matrix = gaussian(splits[8], (RAD, RAD), RAD ** -0.5, 0.375, jnp.float32)
    spectrum = jnp.clip(jnp.exp(math.log(20.0) - 2.9957323 * jax.random.uniform(splits[9], (RAD, AZ), jnp.float32) ** level_of(splits[9], (RAD, AZ), ((0, 64),), -0.2, 0.2)), 1.0, 20.0)
    return {"transmembrane_potential": transmembrane_potential, "channel_openness": channel_openness, "longitudinal_conductance": longitudinal_conductance, "sector_map": sector_map, "cell_index": cell_index, "innervating_neuron": innervating_neuron, "activation_moment": activation_moment, "synapse_position": synapse_position, "radial_basis_matrix": radial_basis_matrix, "spectrum": spectrum}


TIME_STEP = 0.005
G_SODIUM = 120.0
G_POTASSIUM = 36.0
G_LEAK = 0.3
E_SODIUM = 50.0
E_POTASSIUM = -77.0
E_LEAK = -54.4
APPLIED_AMPERES = 800.0


def second_diff(values):
    left_side = jnp.concatenate([values[:, :1], values[:, :-1]], 1)
    right_side = jnp.concatenate([values[:, 1:], values[:, -1:]], 1)
    return left_side + right_side - 2.0 * values


def sarcolemma_model(transmembrane_potential, channel_openness, longitudinal_conductance, activation_substep_count, synapse_position):
    points = lax.broadcasted_iota(jnp.int32, transmembrane_potential.shape, 1)
    destination_position = (points == synapse_position[:, None]).astype(jnp.float32)

    def substep(present_substep_counter, state_pair):
        volt_now, gate_now = state_pair
        membrane_mv = 100.0 * volt_now
        ionic = (G_SODIUM * gate_now[0] ** 3 * gate_now[1] * (membrane_mv - E_SODIUM)
                 + G_POTASSIUM * gate_now[2] ** 4 * (membrane_mv - E_POTASSIUM)
                 + G_LEAK * (membrane_mv - E_LEAK))
        activation_markers = (present_substep_counter >= activation_substep_count)[:, None].astype(jnp.float32)
        applied_excitation = APPLIED_AMPERES * destination_position * activation_markers
        opening = jnp.stack([jax.nn.softplus((membrane_mv + 40.0) / 10.0),
                             0.07 * jnp.exp(-(membrane_mv + 65.0) / 20.0),
                             0.1 * jax.nn.softplus((membrane_mv + 55.0) / 10.0)])
        closing = jnp.stack([4.0 * jnp.exp(-(membrane_mv + 65.0) / 18.0),
                             jax.nn.sigmoid((membrane_mv + 35.0) / 10.0),
                             0.125 * jnp.exp(-(membrane_mv + 65.0) / 80.0)])
        rate_sum = opening + closing
        steady = opening / rate_sum
        gate_after = steady + (gate_now - steady) * jnp.exp(-TIME_STEP * rate_sum)
        volt_after = volt_now + longitudinal_conductance[:, None] * second_diff(volt_now) + (TIME_STEP / 100.0) * (applied_excitation - ionic)
        return volt_after, gate_after

    return lax.fori_loop(0, SUBSTEPS, substep, (transmembrane_potential, channel_openness))


def reference(transmembrane_potential, channel_openness, longitudinal_conductance, sector_map, cell_index, innervating_neuron, activation_moment, synapse_position, radial_basis_matrix, spectrum):
    activation_substep_count = activation_moment[innervating_neuron]
    transmembrane_potential_later, channel_openness_later = sarcolemma_model(transmembrane_potential, channel_openness, longitudinal_conductance, activation_substep_count, synapse_position)
    source = longitudinal_conductance[:, None] * second_diff(transmembrane_potential_later)
    sector_width = AZ // N_SEC
    band_rows = RAD // N_RAD
    fibre_index = jnp.arange(FIBRES, dtype=jnp.int32)
    band_index = (fibre_index // FIB_DEV) % N_RAD
    azimuth = sector_map[:, 0] * sector_width + cell_index // band_rows
    radius = band_index * band_rows + cell_index % band_rows
    source_grid = jnp.zeros((AZ, RAD, AXIAL), jnp.float32).at[azimuth, radius].add(source)
    projected = jnp.einsum("arx,rj->ajx", source_grid, radial_basis_matrix, precision=lax.Precision.HIGHEST)
    spectral = jnp.fft.fft(projected, axis=0, norm="ortho")
    mode_scale = spectrum[:, None, :]
    real_part = jnp.transpose(spectral.real, (1, 2, 0)) * mode_scale
    imag_part = jnp.transpose(spectral.imag, (1, 2, 0)) * mode_scale
    potential = jnp.stack([real_part, imag_part], 2).astype(jnp.float32)
    return transmembrane_potential_later, channel_openness_later, potential
```

```python
import functools
import math

import jax
import jax.numpy as jnp
import numpy as np
from jax import lax
from jax.experimental import pallas as pl
from jax.experimental.pallas import tpu as pltpu
from jax.sharding import PartitionSpec as P

F32 = jnp.float32
BF16 = jnp.bfloat16
MESH = pl.DeviceIdType.MESH

AZ = 512
SUBSTEPS = 10
SEC = 64
RADN = 8
FIB = 128
ROWS = 32


def split2(x):
    hi = x.astype(BF16)
    return hi, (x - hi.astype(F32)).astype(BF16)


def split3(x):
    hi = x.astype(BF16)
    rest = x - hi.astype(F32)
    mid = rest.astype(BF16)
    return hi, mid, (rest - mid.astype(F32)).astype(BF16)


def mxu(a, b, dims=((1,), (0,))):
    return lax.dot_general(a, b, (dims, ((), ())), preferred_element_type=F32)


def iota(shape, dim):
    return lax.broadcasted_iota(jnp.int32, shape, dim)


def inverse(x):
    return pltpu.reciprocal(x, approx=True)


def membrane(k, v, m, h, n, left, right, cond, onset):
    e80 = jnp.exp(jnp.minimum(v * (-100.0 / 80.0) + (-65.0 / 80.0), 10.0))
    e40 = e80 * e80
    e20 = e40 * e40
    e10 = e20 * e20
    close_m = jnp.exp(v * (-100.0 / 18.0) + (-65.0 / 18.0 + math.log(4.0)))
    open_h = 0.07 * e20
    close_n = 0.125 * e80
    open_m = jnp.maximum(v * 10.0 + 4.0 + jnp.log(1.0 + e10 * math.exp(2.5)), 0.0)
    open_n = jnp.maximum(v + 0.55 + 0.1 * jnp.log(1.0 + e10 * math.exp(1.0)), 0.0)
    close_h = inverse(1.0 + e10 * math.exp(3.0))
    gates = []
    for gate, opening, closing in (
        (m, open_m, close_m),
        (h, open_h, close_h),
        (n, open_n, close_n),
    ):
        rate = opening + closing
        steady = opening * inverse(rate)
        gates.append(steady + (gate - steady) * jnp.exp(rate * -0.005))
    nn = n * n
    ionic = (
        (m * m * m * h) * (0.6 * v - 0.3)
        + (nn * nn) * (0.18 * v + 0.1386)
        + (0.0015 * v + 0.000816)
    )
    stimulus = jnp.where(onset <= float(k), 0.04, 0.0)
    after = v + cond * (left + right - 2.0 * v) + (stimulus - ionic)
    return [after] + gates


def neighbours(low, high, first, last):
    up_low, up_high = pltpu.roll(low, 1, 1), pltpu.roll(high, 1, 1)
    down_low, down_high = pltpu.roll(low, 127, 1), pltpu.roll(high, 127, 1)
    return (
        jnp.where(first, low, up_low),
        jnp.where(first, up_low, up_high),
        jnp.where(last, down_high, down_low),
        jnp.where(last, high, down_high),
    )


def exchange_kernel(
    v_hbm,
    gates_hbm,
    basis_hbm,
    cond_ref,
    sector_ref,
    cell_ref,
    neuron_ref,
    moment_ref,
    synapse_ref,
    v_out,
    gates_out,
    all_out,
    v_in,
    gates_in,
    basis,
    v_new,
    gates_new,
    cols,
    src,
    placed,
    got_fibres,
    big_hi,
    big_lo,
    slabs,
    field,
    projected,
    got_all,
    load_sem,
    basis_sem,
    store_sem,
    send_sem,
    local_sem,
    got_sem,
):
    me = lax.axis_index("sec")
    band = lax.axis_index("rad")

    loads = [
        pltpu.make_async_copy(v_hbm, v_in, load_sem.at[0]),
        pltpu.make_async_copy(gates_hbm, gates_in, load_sem.at[1]),
    ]
    for c in loads:
        c.start()
    load_basis = pltpu.make_async_copy(basis_hbm, basis, basis_sem)
    load_basis.start()

    barrier = pltpu.get_barrier_semaphore()

    def greet(i, carry):
        pl.semaphore_signal(
            barrier, inc=1, device_id={"sec": lax.rem(me + i, SEC)}, device_id_type=MESH
        )
        return carry

    lax.fori_loop(1, SEC, greet, 0)
    for i in range(1, RADN):
        pl.semaphore_signal(
            barrier, inc=1, device_id={"rad": lax.rem(band + i, RADN)}, device_id_type=MESH
        )

    sector_row = sector_ref[...].astype(F32)
    cell = cell_ref[...]
    azimuth = cell // 32
    code_row = ((azimuth % 4) * 64 + (azimuth // 4) * 32 + cell % 32 + 1).astype(F32)
    stacked = jnp.concatenate(
        [
            cond_ref[...],
            synapse_ref[...].astype(F32),
            neuron_ref[...].astype(F32),
            sector_row,
            code_row,
            jnp.zeros((123, FIB), F32),
        ],
        0,
    )
    as_cols = stacked.T
    unit = iota((FIB, 512), 1).astype(F32)
    moments = moment_ref[...].astype(F32)
    onset_col = jnp.sum(jnp.where(as_cols[:, 2:3] == unit, moments, 0.0), 1, keepdims=True)
    lane = iota((FIB, FIB), 1)
    cols[...] = jnp.where(lane == 2, onset_col, as_cols)
    same = (as_cols[:, 3:4] == sector_row) & (iota((FIB, FIB), 0) < lane)
    rank_row = jnp.sum(jnp.where(same, 1.0, 0.0), 0, keepdims=True)
    slot_row = sector_row * 8.0 + rank_row
    slot = iota((512, FIB), 0).astype(F32)
    into_slots = jnp.concatenate(
        [
            jnp.where(slot == slot_row, 1.0, 0.0).astype(BF16),
            jnp.where(slot == slot_row + 4.0, 1.0, 0.0).astype(BF16),
        ],
        1,
    )

    for c in loads:
        c.wait()

    def fibres(i, carry):
        rows = pl.ds(pl.multiple_of(i * ROWS, ROWS), ROWS)
        points = iota((ROWS, 128), 1)
        first, last = points == 0, points == 127
        info = cols[rows, :]
        cond = jnp.broadcast_to(info[:, 0:1], (ROWS, 128))
        synapse, onset = info[:, 1:2], info[:, 2:3]
        state, onsets = [], []
        for half in range(2):
            at = slice(128 * half, 128 * half + 128)
            state.append([v_in[rows, at]] + [gates_in[q, rows, at] for q in range(3)])
            onsets.append(
                jnp.where((points + 128 * half).astype(F32) == synapse, onset, 1e9)
            )
        for k in range(SUBSTEPS):
            l0, l1, r0, r1 = neighbours(state[0][0], state[1][0], first, last)
            state = [
                membrane(k, *state[0], l0, r0, cond, onsets[0]),
                membrane(k, *state[1], l1, r1, cond, onsets[1]),
            ]
        for half in range(2):
            at = slice(128 * half, 128 * half + 128)
            v_new[rows, at] = state[half][0]
            for q in range(3):
                gates_new[q, rows, at] = state[half][1 + q]
        l0, l1, r0, r1 = neighbours(state[0][0], state[1][0], first, last)
        src[rows, :] = cond * (l0 + r0 - 2.0 * state[0][0])
        high = cond * (l1 + r1 - 2.0 * state[1][0])
        src[pl.ds(pl.multiple_of(FIB + i * ROWS, ROWS), ROWS), :] = jnp.where(
            last, info[:, 4:5], high
        )
        return carry

    lax.fori_loop(0, FIB // ROWS, fibres, 0)

    stores = [
        pltpu.make_async_copy(v_new, v_out, store_sem.at[0]),
        pltpu.make_async_copy(gates_new, gates_out, store_sem.at[1]),
    ]
    for c in stores:
        c.start()

    s_hi, s_mid, s_lo = split3(src[...])
    placed[...] = mxu(into_slots, s_hi) + mxu(into_slots, s_mid) + mxu(into_slots, s_lo)

    pl.semaphore_wait(barrier, SEC + RADN - 2)

    def over_sectors(source, target, n):
        def send(i, carry):
            d = lax.rem(me + i, SEC)
            pltpu.make_async_remote_copy(
                source.at[pl.ds(pl.multiple_of(d * 8, 8), 8)],
                target.at[pl.ds(pl.multiple_of(me * 8, 8), 8)],
                send_sem.at[n],
                got_sem.at[n],
                device_id={"sec": d},
                device_id_type=MESH,
            ).start()
            return carry

        lax.fori_loop(1, SEC, send, 0)
        own = pl.ds(pl.multiple_of(me * 8, 8), 8)
        local = pltpu.make_async_copy(source.at[own], target.at[own], local_sem.at[n])
        local.start()
        return local

    def all_of(buffer, sem):
        pltpu.make_async_copy(buffer, buffer, sem).wait()

    local1 = over_sectors(placed, got_fibres, 0)

    load_basis.wait()
    b_hi, b_lo = split2(basis[...])
    row, col = iota((512, 256), 0), iota((512, 256), 1)
    for half in range(2):
        pick = jnp.where(
            ((row // 8) * 4 + row % 4 == col) & ((row % 8) // 4 == half), 1.0, 0.0
        ).astype(BF16)
        at = slice(256 * half, 256 * half + 256)
        big_hi[:, at] = mxu(pick, b_hi, ((1,), (1,))).astype(BF16)
        big_lo[:, at] = mxu(pick, b_lo, ((1,), (1,))).astype(BF16)

    most = pl.ds(0, 8 * (SEC - 1))
    all_of(got_fibres.at[most], got_sem.at[0])
    local1.wait()

    x = got_fibres[...]
    end = iota((8, 128), 1) == 127
    codes = mxu(jnp.where(end, 1.0, 0.0).astype(BF16), x.astype(BF16), ((1,), (1,)))
    slots = iota((8, 512), 1)
    upper = slots % 8 >= 4
    codes = jnp.where(upper, codes + 256.0, pltpu.roll(codes, 508, 1)) - 1.0
    into_cells = jnp.where(iota((512, 512), 0).astype(F32) == codes[0:1], 1.0, 0.0).astype(BF16)
    rows8 = iota((512, 128), 0) % 8
    coded = (rows8 >= 4) & (iota((512, 128), 1) == 127)
    x = jnp.where(coded, 0.0, x)
    sums = jnp.sum(x, 1, keepdims=True)
    sums = sums + pltpu.roll(jnp.broadcast_to(sums, (512, 128)), 4, 0)
    x = jnp.where(coded, -sums, x)
    x_hi, x_lo = split2(x)
    cells = mxu(into_cells, x_hi) + mxu(into_cells, x_lo)

    lanes = iota((64, 128), 1)
    wide, odd = lanes >= 64, lanes % 64 >= 32
    for half in range(2):
        t = [cells[256 * half + 64 * a : 256 * half + 64 * a + 64] for a in range(4)]
        for a in range(2):
            p, q = t[a], t[a + 2]
            t[a] = jnp.where(wide, pltpu.roll(q, 64, 1), p)
            t[a + 2] = jnp.where(wide, q, pltpu.roll(p, 64, 1))
        for a in (0, 2):
            p, q = t[a], t[a + 1]
            t[a] = jnp.where(odd, pltpu.roll(q, 32, 1), p)
            t[a + 1] = jnp.where(odd, q, pltpu.roll(p, 96, 1))
        for b in range(4):
            slabs[4 * half + b] = t[b].reshape(2, 32, 128)

    for i in range(1, RADN):
        d = lax.rem(band + i, RADN)
        pltpu.make_async_remote_copy(
            slabs.at[d],
            field.at[:, band],
            send_sem.at[1],
            got_sem.at[1],
            device_id={"rad": d},
            device_id_type=MESH,
        ).start()
    local2 = pltpu.make_async_copy(slabs.at[band], field.at[:, band], local_sem.at[1])
    local2.start()
    all_of(field.at[:, pl.ds(0, RADN - 1)], got_sem.at[1])
    local2.wait()

    f_hi, f_lo = split2(field[...].reshape(512, 128))
    projected[...] = mxu(big_hi[...], f_hi) + mxu(big_hi[...], f_lo) + mxu(big_lo[...], f_hi)
    local3 = over_sectors(projected, got_all, 2)
    for c in stores:
        c.wait()
    all_of(placed.at[most], send_sem.at[0])
    all_of(slabs.at[pl.ds(0, RADN - 1)], send_sem.at[1])
    all_of(got_all.at[most], got_sem.at[2])
    local3.wait()
    all_out[...] = got_all[...]
    all_of(projected.at[most], send_sem.at[2])


def spectral_kernel(
    all_ref, table_hi, table_lo, spectrum_ref, v_hbm, gates_hbm, out_ref, v_out, gates_out, sem
):
    passed = [
        pltpu.make_async_copy(v_hbm, v_out, sem.at[0]),
        pltpu.make_async_copy(gates_hbm, gates_out, sem.at[1]),
    ]
    for c in passed:
        c.start()
    parts = []
    for j in range(4):
        z = all_ref[pl.ds(j, 128, stride=4), :].T
        parts.append(jnp.concatenate([z[32 * a : 32 * a + 32] for a in range(4)], 1))
    hi, lo = split2(jnp.concatenate(parts, 0))
    for tile in range(4):
        at = slice(128 * tile, 128 * tile + 128)
        scale = jnp.concatenate(
            [jnp.broadcast_to(spectrum_ref[j : j + 1, at], (32, 128)) for j in range(4)], 0
        )
        for part in range(2):
            to = slice(512 * part + 128 * tile, 512 * part + 128 * tile + 128)
            y = mxu(hi, table_hi[:, to]) + mxu(lo, table_hi[:, to]) + mxu(hi, table_lo[:, to])
            out_ref[pl.ds(2 * tile + part, 128, stride=8), :] = y * scale
    for c in passed:
        c.wait()


def azimuth_table():
    low, rest = np.meshgrid(np.arange(4), np.arange(128), indexing="ij")
    azimuth = (rest * 4 + low).reshape(-1)
    phase = (azimuth[:, None] * np.arange(AZ)[None, :] % AZ) * (2.0 * math.pi / AZ)
    table = np.concatenate([np.cos(phase), -np.sin(phase)], 1) / math.sqrt(AZ)
    hi = table.astype(np.float32).astype(jnp.bfloat16)
    lo = (table - hi.astype(np.float64)).astype(np.float32).astype(jnp.bfloat16)
    return hi, lo


def per_device(
    voltage,
    gates,
    conductance,
    sector_map,
    cell_index,
    neuron,
    moment,
    synapse,
    basis,
    spectrum,
):
    any_space = pl.BlockSpec(memory_space=pl.ANY)
    vmem = pl.BlockSpec(memory_space=pltpu.VMEM)
    v_later, gates_later, everything = pl.pallas_call(
        exchange_kernel,
        out_shape=[
            jax.ShapeDtypeStruct((FIB, 256), F32),
            jax.ShapeDtypeStruct((3, FIB, 256), F32),
            jax.ShapeDtypeStruct((512, 128), F32),
        ],
        in_specs=[any_space] * 3 + [vmem] * 6,
        out_specs=[any_space, any_space, vmem],
        scratch_shapes=[
            pltpu.VMEM((FIB, 256), F32),
            pltpu.VMEM((3, FIB, 256), F32),
            pltpu.VMEM((256, 256), F32),
            pltpu.VMEM((FIB, 256), F32),
            pltpu.VMEM((3, FIB, 256), F32),
            pltpu.VMEM((FIB, 128), F32),
            pltpu.VMEM((2 * FIB, 128), F32),
            pltpu.VMEM((512, 128), F32),
            pltpu.VMEM((512, 128), F32),
            pltpu.VMEM((512, 512), BF16),
            pltpu.VMEM((512, 512), BF16),
            pltpu.VMEM((8, 2, 32, 128), F32),
            pltpu.VMEM((2, 8, 32, 128), F32),
            pltpu.VMEM((512, 128), F32),
            pltpu.VMEM((512, 128), F32),
            pltpu.SemaphoreType.DMA((2,)),
            pltpu.SemaphoreType.DMA,
            pltpu.SemaphoreType.DMA((2,)),
            pltpu.SemaphoreType.DMA((3,)),
            pltpu.SemaphoreType.DMA((3,)),
            pltpu.SemaphoreType.DMA((3,)),
        ],
        compiler_params=pltpu.CompilerParams(
            collective_id=0, has_side_effects=True, vmem_limit_bytes=32 << 20
        ),
    )(
        voltage,
        gates,
        basis,
        conductance.reshape(1, FIB),
        sector_map.reshape(1, FIB),
        cell_index.reshape(1, FIB),
        neuron.reshape(1, FIB),
        moment.reshape(1, 512),
        synapse.reshape(1, FIB),
    )
    table_hi, table_lo = azimuth_table()
    tiles, v_final, gates_final = pl.pallas_call(
        spectral_kernel,
        out_shape=[
            jax.ShapeDtypeStruct((1024, 128), F32),
            jax.ShapeDtypeStruct((FIB, 256), F32),
            jax.ShapeDtypeStruct((3, FIB, 256), F32),
        ],
        in_specs=[vmem] * 4 + [any_space] * 2,
        out_specs=[vmem, any_space, any_space],
        scratch_shapes=[pltpu.SemaphoreType.DMA((2,))],
        compiler_params=pltpu.CompilerParams(vmem_limit_bytes=32 << 20),
    )(
        everything,
        jnp.asarray(table_hi),
        jnp.asarray(table_lo),
        spectrum,
        v_later,
        gates_later,
    )
    potential = tiles.reshape(4, 32, 4, 2, 128).transpose(0, 1, 3, 2, 4).reshape(4, 32, 2, AZ)
    return v_final, gates_final, potential


def solution(mesh):
    placed = (
        P(("sec", "rad"), None),
        P(None, ("sec", "rad"), None),
        P(("sec", "rad")),
        P(("sec", "rad"), None),
        P(("sec", "rad")),
        P(("sec", "rad")),
        P(),
        P(("sec", "rad")),
        P(),
        P("sec", None),
    )
    return jax.shard_map(
        per_device,
        mesh=mesh,
        in_specs=placed,
        out_specs=(
            P(("sec", "rad"), None),
            P(None, ("sec", "rad"), None),
            P("sec", "rad", None, None),
        ),
        check_vma=False,
    )
```

```python
import functools
import math

import jax
import jax.numpy as jnp
import numpy as np
from jax import lax
from jax.experimental import pallas as pl
from jax.experimental.pallas import tpu as pltpu
from jax.sharding import PartitionSpec as P

F32 = jnp.float32
BF16 = jnp.bfloat16
MESH = pl.DeviceIdType.MESH

AZ = 512
SUBSTEPS = 10
SEC = 64
RADN = 8
FIB = 128
ROWS = 32


def split2(x):
    hi = x.astype(BF16)
    return hi, (x - hi.astype(F32)).astype(BF16)


def split3(x):
    hi = x.astype(BF16)
    rest = x - hi.astype(F32)
    mid = rest.astype(BF16)
    return hi, mid, (rest - mid.astype(F32)).astype(BF16)


def mxu(a, b, dims=((1,), (0,))):
    return lax.dot_general(a, b, (dims, ((), ())), preferred_element_type=F32)


def iota(shape, dim):
    return lax.broadcasted_iota(jnp.int32, shape, dim)


def inverse(x):
    return pltpu.reciprocal(x, approx=True)


def membrane(k, v, m, h, n, left, right, cond, onset):
    e80 = jnp.exp(jnp.minimum(v * (-100.0 / 80.0) + (-65.0 / 80.0), 10.0))
    e40 = e80 * e80
    e20 = e40 * e40
    e10 = e20 * e20
    close_m = jnp.exp(v * (-100.0 / 18.0) + (-65.0 / 18.0 + math.log(4.0)))
    open_h = 0.07 * e20
    close_n = 0.125 * e80
    open_m = jnp.maximum(v * 10.0 + 4.0 + jnp.log(1.0 + e10 * math.exp(2.5)), 0.0)
    open_n = jnp.maximum(v + 0.55 + 0.1 * jnp.log(1.0 + e10 * math.exp(1.0)), 0.0)
    close_h = inverse(1.0 + e10 * math.exp(3.0))
    gates = []
    for gate, opening, closing in (
        (m, open_m, close_m),
        (h, open_h, close_h),
        (n, open_n, close_n),
    ):
        rate = opening + closing
        steady = opening * inverse(rate)
        gates.append(steady + (gate - steady) * jnp.exp(rate * -0.005))
    nn = n * n
    ionic = (
        (m * m * m * h) * (0.6 * v - 0.3)
        + (nn * nn) * (0.18 * v + 0.1386)
        + (0.0015 * v + 0.000816)
    )
    stimulus = jnp.where(onset <= float(k), 0.04, 0.0)
    after = v + cond * (left + right - 2.0 * v) + (stimulus - ionic)
    return [after] + gates


def neighbours(low, high, first, last):
    up_low, up_high = pltpu.roll(low, 1, 1), pltpu.roll(high, 1, 1)
    down_low, down_high = pltpu.roll(low, 127, 1), pltpu.roll(high, 127, 1)
    return (
        jnp.where(first, low, up_low),
        jnp.where(first, up_low, up_high),
        jnp.where(last, down_high, down_low),
        jnp.where(last, high, down_high),
    )


def exchange_kernel(
    v_hbm,
    gates_hbm,
    basis_hbm,
    cond_hbm,
    sector_hbm,
    cell_hbm,
    neuron_hbm,
    moment_hbm,
    synapse_hbm,
    v_out,
    gates_out,
    all_out,
    v_in,
    gates_in,
    basis,
    cond_ref,
    sector_ref,
    cell_ref,
    neuron_ref,
    moment_ref,
    synapse_ref,
    v_new,
    gates_new,
    cols,
    src,
    codes_out,
    codes_in,
    placed,
    got_fibres,
    slabs,
    field,
    projected,
    got_all,
    load_sem,
    small_sem,
    basis_sem,
    store_sem,
    send_sem,
    local_sem,
    got_sem,
):
    me = lax.axis_index("sec")
    band = lax.axis_index("rad")

    loads = [
        pltpu.make_async_copy(v_hbm, v_in, load_sem.at[0]),
        pltpu.make_async_copy(gates_hbm, gates_in, load_sem.at[1]),
    ]
    for c in loads:
        c.start()
    small = [
        pltpu.make_async_copy(a, b, small_sem.at[i])
        for i, (a, b) in enumerate(
            [
                (cond_hbm, cond_ref),
                (sector_hbm, sector_ref),
                (cell_hbm, cell_ref),
                (neuron_hbm, neuron_ref),
                (moment_hbm, moment_ref),
                (synapse_hbm, synapse_ref),
            ]
        )
    ]
    for c in small:
        c.start()
    load_basis = pltpu.make_async_copy(basis_hbm, basis, basis_sem)
    load_basis.start()

    barrier = pltpu.get_barrier_semaphore()

    def greet(i, carry):
        pl.semaphore_signal(
            barrier, inc=1, device_id={"sec": lax.rem(me + i, SEC)}, device_id_type=MESH
        )
        return carry

    lax.fori_loop(1, SEC, greet, 0)
    for i in range(1, RADN):
        pl.semaphore_signal(
            barrier, inc=1, device_id={"rad": lax.rem(band + i, RADN)}, device_id_type=MESH
        )

    for c in small:
        c.wait()
    sector_row = sector_ref[...].astype(F32)
    stacked = jnp.concatenate(
        [
            cond_ref[...],
            synapse_ref[...].astype(F32),
            neuron_ref[...].astype(F32),
            sector_row,
            cell_ref[...].astype(F32),
            jnp.zeros((123, FIB), F32),
        ],
        0,
    )
    as_cols = stacked.T
    unit = iota((FIB, 512), 1).astype(F32)
    moments = moment_ref[...].astype(F32)
    onset_col = jnp.sum(jnp.where(as_cols[:, 2:3] == unit, moments, 0.0), 1, keepdims=True)
    line, lane = iota((FIB, FIB), 0), iota((FIB, FIB), 1)
    cols[...] = jnp.where(lane == 2, onset_col, as_cols)
    same = as_cols[:, 3:4] == sector_row
    rank_row = jnp.sum(jnp.where(same & (line < lane), 1.0, 0.0), 0, keepdims=True)
    rank_col = jnp.sum(jnp.where(same & (lane < line), 1.0, 0.0), 1, keepdims=True)
    slot = iota((256, FIB), 0).astype(F32)
    into_slots = jnp.where(slot == sector_row * 4.0 + rank_row, 1.0, 0.0).astype(BF16)
    into_sectors = jnp.where(iota((SEC, FIB), 0).astype(F32) == sector_row, 1.0, 0.0)
    at_lane = (lane - 4 * lax.rem(me, 32)).astype(F32) == rank_col
    codes_out[...] = mxu(
        into_sectors.astype(BF16), jnp.where(at_lane, as_cols[:, 4:5] + 1.0, 0.0).astype(BF16)
    )

    for c in loads:
        c.wait()

    def fibres(i, carry):
        rows = pl.ds(pl.multiple_of(i * ROWS, ROWS), ROWS)
        points = iota((ROWS, 128), 1)
        first, last = points == 0, points == 127
        info = cols[rows, :]
        cond = jnp.broadcast_to(info[:, 0:1], (ROWS, 128))
        synapse, onset = info[:, 1:2], info[:, 2:3]
        state, onsets = [], []
        for half in range(2):
            at = slice(128 * half, 128 * half + 128)
            state.append([v_in[rows, at]] + [gates_in[q, rows, at] for q in range(3)])
            onsets.append(
                jnp.where((points + 128 * half).astype(F32) == synapse, onset, 1e9)
            )
        for k in range(SUBSTEPS):
            l0, l1, r0, r1 = neighbours(state[0][0], state[1][0], first, last)
            state = [
                membrane(k, *state[0], l0, r0, cond, onsets[0]),
                membrane(k, *state[1], l1, r1, cond, onsets[1]),
            ]
        for half in range(2):
            at = slice(128 * half, 128 * half + 128)
            v_new[rows, at] = state[half][0]
            for q in range(3):
                gates_new[q, rows, at] = state[half][1 + q]
        l0, l1, r0, r1 = neighbours(state[0][0], state[1][0], first, last)
        low = cond * (l0 + r0 - 2.0 * state[0][0])
        high = cond * (l1 + r1 - 2.0 * state[1][0])
        even = points % 32 < 16
        src[0, rows, :] = jnp.where(even, low, pltpu.roll(high, 16, 1))
        src[1, rows, :] = jnp.where(even, pltpu.roll(low, 112, 1), high)
        return carry

    lax.fori_loop(0, FIB // ROWS, fibres, 0)

    stores = [
        pltpu.make_async_copy(v_new, v_out, store_sem.at[0]),
        pltpu.make_async_copy(gates_new, gates_out, store_sem.at[1]),
    ]
    for c in stores:
        c.start()

    for c in range(2):
        s_hi, s_mid, s_lo = split3(src[c])
        placed[c] = mxu(into_slots, s_hi) + mxu(into_slots, s_mid) + mxu(into_slots, s_lo)

    pl.semaphore_wait(barrier, SEC + RADN - 2)

    y, z = me // 16, lax.rem(me, 16)

    def over_sectors(source, target, n, rows):
        own = pl.ds(pl.multiple_of(me * rows, rows), rows)

        def send(to_y, to_z):
            d = lax.rem(y + to_y, 4) * 16 + lax.rem(z + to_z, 16)
            pltpu.make_async_remote_copy(
                source.at[pl.ds(pl.multiple_of(d * rows, rows), rows)],
                target.at[own],
                send_sem.at[n],
                got_sem.at[n],
                device_id={"sec": d},
                device_id_type=MESH,
            ).start()

        def send_far(i, carry):
            away = 8 - (i + 1) // 2
            to_z = jnp.where(lax.rem(i, 2) == 1, away, 16 - away)
            for to_y in (2, 1, 3, 0):
                send(to_y, to_z)
            return carry

        lax.fori_loop(0, 15, send_far, 0)
        for to_y in (2, 1, 3):
            send(to_y, 0)
        local = pltpu.make_async_copy(source.at[own], target.at[own], local_sem.at[n])
        local.start()
        return local

    def all_of(buffer, sem):
        pltpu.make_async_copy(buffer, buffer, sem).wait()

    most = pl.ds(0, SEC - 1)
    most4 = pl.ds(0, 4 * (SEC - 1))
    local_codes = over_sectors(codes_out, codes_in, 0, 1)
    local_fibres = [
        over_sectors(placed.at[c], got_fibres.at[c], 1 + c, 4) for c in range(2)
    ]

    load_basis.wait()
    b_hi, b_lo = split2(basis[...].T)

    all_of(codes_in.at[most], got_sem.at[0])
    local_codes.wait()
    codes = jnp.concatenate(
        [
            jnp.sum(codes_in[0:32, :], 0, keepdims=True),
            jnp.sum(codes_in[32:64, :], 0, keepdims=True),
        ],
        1,
    )
    into_cells = jnp.where(iota((256, 256), 0).astype(F32) + 1.0 == codes, 1.0, 0.0).astype(BF16)

    lanes = iota((32, 128), 1)

    def deposit(c):
        all_of(got_fibres.at[c, most4], got_sem.at[1 + c])
        local_fibres[c].wait()
        x_hi, x_lo = split2(got_fibres[c])
        cells = mxu(into_cells, x_hi) + mxu(into_cells, x_lo)
        t = [cells[32 * a : 32 * a + 32] for a in range(8)]
        for step in (4, 2, 1):
            width = 16 * step
            late = lanes % (2 * width) >= width
            for a in range(8):
                if a // step % 2 == 0:
                    p, q = t[a], t[a + step]
                    t[a] = jnp.where(late, pltpu.roll(q, width, 1), p)
                    t[a + step] = jnp.where(late, q, pltpu.roll(p, 128 - width, 1))
        for q in range(8):
            slabs[c, q // 2 + 4 * (q % 2)] = t[q]
        for i in range(1, RADN):
            d = lax.rem(band + i, RADN)
            pltpu.make_async_remote_copy(
                slabs.at[c, d],
                field.at[c, band],
                send_sem.at[3 + c],
                got_sem.at[3 + c],
                device_id={"rad": d},
                device_id_type=MESH,
            ).start()
        local = pltpu.make_async_copy(slabs.at[c, band], field.at[c, band], local_sem.at[3 + c])
        local.start()
        return local

    def project(c, local):
        all_of(field.at[c, pl.ds(0, RADN - 1)], got_sem.at[3 + c])
        local.wait()
        f_hi, f_lo = split2(field[c].reshape(256, 128))
        projected[c] = mxu(b_hi, f_hi) + mxu(b_hi, f_lo) + mxu(b_lo, f_hi)
        return over_sectors(projected.at[c], got_all.at[c], 5 + c, 4)

    last_copies = []
    for c in range(2):
        last_copies.append(project(c, deposit(c)))

    for c in stores:
        c.wait()
    all_of(codes_out.at[most], send_sem.at[0])
    for c in range(2):
        all_of(placed.at[c, most4], send_sem.at[1 + c])
        all_of(slabs.at[c, pl.ds(0, RADN - 1)], send_sem.at[3 + c])
    for c in range(2):
        all_of(got_all.at[c, most4], got_sem.at[5 + c])
        last_copies[c].wait()
        all_out[c] = got_all[c]
    for c in range(2):
        all_of(projected.at[c, most4], send_sem.at[5 + c])


def spectral_kernel(
    all_ref, table_hi, table_lo, spectrum_ref, v_hbm, gates_hbm, out_ref, v_out, gates_out, sem
):
    passed = [
        pltpu.make_async_copy(v_hbm, v_out, sem.at[0]),
        pltpu.make_async_copy(gates_hbm, gates_out, sem.at[1]),
    ]
    for c in passed:
        c.start()
    parts = []
    near = iota((64, 128), 1) < 64
    for j in range(4):
        first, second = (all_ref[c, pl.ds(j, 64, stride=4), :] for c in range(2))
        lower = jnp.where(near, first, pltpu.roll(second, 64, 1))
        upper = jnp.where(near, pltpu.roll(first, 64, 1), second)
        t = jnp.concatenate([lower, upper], 0).T
        for c in range(2):
            at = [64 * c + 16 * a for a in range(4)]
            parts.append(jnp.concatenate([t[i : i + 16] for i in at], 1))
    hi, lo = split2(jnp.concatenate(parts, 0))
    for tile in range(4):
        at = slice(128 * tile, 128 * tile + 128)
        scale = jnp.concatenate(
            [jnp.broadcast_to(spectrum_ref[j : j + 1, at], (32, 128)) for j in range(4)], 0
        )
        for part in range(2):
            to = slice(512 * part + 128 * tile, 512 * part + 128 * tile + 128)
            y = mxu(hi, table_hi[:, to]) + mxu(lo, table_hi[:, to]) + mxu(hi, table_lo[:, to])
            out_ref[pl.ds(2 * tile + part, 128, stride=8), :] = y * scale
    for c in passed:
        c.wait()


def azimuth_table():
    low, high, sector = np.meshgrid(np.arange(4), np.arange(2), np.arange(SEC), indexing="ij")
    azimuth = (sector * 8 + high * 4 + low).reshape(-1)
    phase = (azimuth[:, None] * np.arange(AZ)[None, :] % AZ) * (2.0 * math.pi / AZ)
    table = np.concatenate([np.cos(phase), -np.sin(phase)], 1) / math.sqrt(AZ)
    hi = table.astype(np.float32).astype(jnp.bfloat16)
    lo = (table - hi.astype(np.float64)).astype(np.float32).astype(jnp.bfloat16)
    return hi, lo


def per_device(
    voltage,
    gates,
    conductance,
    sector_map,
    cell_index,
    neuron,
    moment,
    synapse,
    basis,
    spectrum,
):
    any_space = pl.BlockSpec(memory_space=pl.ANY)
    vmem = pl.BlockSpec(memory_space=pltpu.VMEM)
    hbm = pl.BlockSpec(memory_space=pltpu.HBM)
    v_later, gates_later, everything = pl.pallas_call(
        exchange_kernel,
        out_shape=[
            jax.ShapeDtypeStruct((FIB, 256), F32),
            jax.ShapeDtypeStruct((3, FIB, 256), F32),
            jax.ShapeDtypeStruct((2, 256, 128), F32),
        ],
        in_specs=[hbm] * 9,
        out_specs=[any_space, any_space, vmem],
        scratch_shapes=[
            pltpu.VMEM((FIB, 256), F32),
            pltpu.VMEM((3, FIB, 256), F32),
            pltpu.VMEM((256, 256), F32),
            pltpu.VMEM((1, FIB), F32),
            pltpu.VMEM((1, FIB), jnp.int32),
            pltpu.VMEM((1, FIB), jnp.int32),
            pltpu.VMEM((1, FIB), jnp.int32),
            pltpu.VMEM((1, 512), jnp.int32),
            pltpu.VMEM((1, FIB), jnp.int32),
            pltpu.VMEM((FIB, 256), F32),
            pltpu.VMEM((3, FIB, 256), F32),
            pltpu.VMEM((FIB, 128), F32),
            pltpu.VMEM((2, FIB, 128), F32),
            pltpu.VMEM((SEC, 128), F32),
            pltpu.VMEM((SEC, 128), F32),
            pltpu.VMEM((2, 256, 128), F32),
            pltpu.VMEM((2, 256, 128), F32),
            pltpu.VMEM((2, 8, 32, 128), F32),
            pltpu.VMEM((2, 8, 32, 128), F32),
            pltpu.VMEM((2, 256, 128), F32),
            pltpu.VMEM((2, 256, 128), F32),
            pltpu.SemaphoreType.DMA((2,)),
            pltpu.SemaphoreType.DMA((6,)),
            pltpu.SemaphoreType.DMA,
            pltpu.SemaphoreType.DMA((2,)),
            pltpu.SemaphoreType.DMA((7,)),
            pltpu.SemaphoreType.DMA((7,)),
            pltpu.SemaphoreType.DMA((7,)),
        ],
        compiler_params=pltpu.CompilerParams(
            collective_id=0, has_side_effects=True, vmem_limit_bytes=32 << 20
        ),
        cost_estimate=pl.CostEstimate(
            flops=20_000_000_000, bytes_accessed=100_000_000, transcendentals=4_000_000
        ),
    )(
        *(
            pltpu.with_memory_space_constraint(a, pltpu.HBM)
            for a in (
                voltage,
                gates,
                basis,
                conductance.reshape(1, FIB),
                sector_map.reshape(1, FIB),
                cell_index.reshape(1, FIB),
                neuron.reshape(1, FIB),
                moment.reshape(1, 512),
                synapse.reshape(1, FIB),
            )
        )
    )
    table_hi, table_lo = azimuth_table()
    tiles, v_final, gates_final = pl.pallas_call(
        spectral_kernel,
        out_shape=[
            jax.ShapeDtypeStruct((1024, 128), F32),
            jax.ShapeDtypeStruct((FIB, 256), F32),
            jax.ShapeDtypeStruct((3, FIB, 256), F32),
        ],
        in_specs=[vmem] * 4 + [any_space] * 2,
        out_specs=[vmem, any_space, any_space],
        scratch_shapes=[pltpu.SemaphoreType.DMA((2,))],
        compiler_params=pltpu.CompilerParams(vmem_limit_bytes=32 << 20),
    )(
        everything,
        jnp.asarray(table_hi),
        jnp.asarray(table_lo),
        spectrum,
        v_later,
        gates_later,
    )
    potential = tiles.reshape(4, 32, 4, 2, 128).transpose(0, 1, 3, 2, 4).reshape(4, 32, 2, AZ)
    return v_final, gates_final, potential


def solution(mesh):
    placed = (
        P(("sec", "rad"), None),
        P(None, ("sec", "rad"), None),
        P(("sec", "rad")),
        P(("sec", "rad"), None),
        P(("sec", "rad")),
        P(("sec", "rad")),
        P(),
        P(("sec", "rad")),
        P(),
        P("sec", None),
    )
    return jax.shard_map(
        per_device,
        mesh=mesh,
        in_specs=placed,
        out_specs=(
            P(("sec", "rad"), None),
            P(None, ("sec", "rad"), None),
            P("sec", "rad", None, None),
        ),
        check_vma=False,
    )
```

```python
import functools
import math

import jax
import jax.numpy as jnp
import numpy as np
from jax import lax
from jax.experimental import pallas as pl
from jax.experimental.pallas import tpu as pltpu
from jax.sharding import PartitionSpec as P

F32 = jnp.float32
BF16 = jnp.bfloat16
MESH = pl.DeviceIdType.MESH

AZ = 512
SUBSTEPS = 10
SEC = 64
RADN = 8
FIB = 128
ROWS = 32


def split2(x):
    hi = x.astype(BF16)
    return hi, (x - hi.astype(F32)).astype(BF16)


def split3(x):
    hi = x.astype(BF16)
    rest = x - hi.astype(F32)
    mid = rest.astype(BF16)
    return hi, mid, (rest - mid.astype(F32)).astype(BF16)


def mxu(a, b, dims=((1,), (0,))):
    return lax.dot_general(a, b, (dims, ((), ())), preferred_element_type=F32)


def iota(shape, dim):
    return lax.broadcasted_iota(jnp.int32, shape, dim)


def inverse(x):
    return pltpu.reciprocal(x, approx=True)


def membrane(k, v, m, h, n, left, right, cond, onset):
    e80 = jnp.exp(jnp.minimum(v * (-100.0 / 80.0) + (-65.0 / 80.0), 10.0))
    e40 = e80 * e80
    e20 = e40 * e40
    e10 = e20 * e20
    close_m = jnp.exp(v * (-100.0 / 18.0) + (-65.0 / 18.0 + math.log(4.0)))
    open_h = 0.07 * e20
    close_n = 0.125 * e80
    open_m = jnp.maximum(v * 10.0 + 4.0 + jnp.log(1.0 + e10 * math.exp(2.5)), 0.0)
    open_n = jnp.maximum(v + 0.55 + 0.1 * jnp.log(1.0 + e10 * math.exp(1.0)), 0.0)
    close_h = inverse(1.0 + e10 * math.exp(3.0))
    gates = []
    for gate, opening, closing in (
        (m, open_m, close_m),
        (h, open_h, close_h),
        (n, open_n, close_n),
    ):
        rate = opening + closing
        steady = opening * inverse(rate)
        gates.append(steady + (gate - steady) * jnp.exp(rate * -0.005))
    nn = n * n
    ionic = (
        (m * m * m * h) * (0.6 * v - 0.3)
        + (nn * nn) * (0.18 * v + 0.1386)
        + (0.0015 * v + 0.000816)
    )
    stimulus = jnp.where(onset <= float(k), 0.04, 0.0)
    after = v + cond * (left + right - 2.0 * v) + (stimulus - ionic)
    return [after] + gates


def neighbours(low, high, first, last):
    up_low, up_high = pltpu.roll(low, 1, 1), pltpu.roll(high, 1, 1)
    down_low, down_high = pltpu.roll(low, 127, 1), pltpu.roll(high, 127, 1)
    return (
        jnp.where(first, low, up_low),
        jnp.where(first, up_low, up_high),
        jnp.where(last, down_high, down_low),
        jnp.where(last, high, down_high),
    )


def exchange_kernel(
    v_hbm,
    gates_hbm,
    basis_hbm,
    cond_hbm,
    sector_hbm,
    cell_hbm,
    neuron_hbm,
    moment_hbm,
    synapse_hbm,
    v_out,
    gates_out,
    all_out,
    v_in,
    gates_in,
    basis,
    cond_ref,
    sector_ref,
    cell_ref,
    neuron_ref,
    moment_ref,
    synapse_ref,
    v_new,
    gates_new,
    cols,
    src,
    codes_out,
    codes_in,
    placed,
    got_fibres,
    slabs,
    field,
    projected,
    got_all,
    load_sem,
    small_sem,
    basis_sem,
    store_sem,
    send_sem,
    local_sem,
    got_sem,
):
    me = lax.axis_index("sec")
    band = lax.axis_index("rad")

    loads = [
        pltpu.make_async_copy(v_hbm, v_in, load_sem.at[0]),
        pltpu.make_async_copy(gates_hbm, gates_in, load_sem.at[1]),
    ]
    for c in loads:
        c.start()
    small = [
        pltpu.make_async_copy(a, b, small_sem.at[i])
        for i, (a, b) in enumerate(
            [
                (cond_hbm, cond_ref),
                (sector_hbm, sector_ref),
                (cell_hbm, cell_ref),
                (neuron_hbm, neuron_ref),
                (moment_hbm, moment_ref),
                (synapse_hbm, synapse_ref),
            ]
        )
    ]
    for c in small:
        c.start()
    load_basis = pltpu.make_async_copy(basis_hbm, basis, basis_sem)
    load_basis.start()

    barrier = pltpu.get_barrier_semaphore()

    y, z = me // 16, lax.rem(me, 16)

    def over_partners(act):
        def far(i, carry):
            away = 8 - (i + 1) // 2
            to_z = lax.rem(z + jnp.where(lax.rem(i, 2) == 1, away, 16 - away), 16)
            for to_y in (2, 1, 3, 0):
                act(lax.rem(y + to_y, 4) * 16 + to_z)
            return carry

        lax.fori_loop(0, 15, far, 0)
        for to_y in (2, 1, 3):
            act(lax.rem(y + to_y, 4) * 16 + z)

    def over_partners_in_order(act):
        def at_z(to_z, carry):
            for to_y in (2, 1, 3):
                act(lax.rem(y + to_y, 4) * 16 + to_z)

            @pl.when(to_z != z)
            def _():
                act(y * 16 + to_z)

            return carry

        lax.fori_loop(0, 16, at_z, 0)

    over_partners(
        lambda d: pl.semaphore_signal(
            barrier, inc=1, device_id={"sec": d}, device_id_type=MESH
        )
    )
    for i in range(1, RADN):
        pl.semaphore_signal(
            barrier, inc=1, device_id={"rad": lax.rem(band + i, RADN)}, device_id_type=MESH
        )

    for c in small:
        c.wait()
    sector_row = sector_ref[...].astype(F32)
    stacked = jnp.concatenate(
        [
            cond_ref[...],
            synapse_ref[...].astype(F32),
            neuron_ref[...].astype(F32),
            sector_row,
            cell_ref[...].astype(F32),
            jnp.zeros((123, FIB), F32),
        ],
        0,
    )
    as_cols = stacked.T
    unit = iota((FIB, 512), 1).astype(F32)
    moments = moment_ref[...].astype(F32)
    onset_col = jnp.sum(jnp.where(as_cols[:, 2:3] == unit, moments, 0.0), 1, keepdims=True)
    line, lane = iota((FIB, FIB), 0), iota((FIB, FIB), 1)
    cols[...] = jnp.where(lane == 2, onset_col, as_cols)
    same = as_cols[:, 3:4] == sector_row
    rank_row = jnp.sum(jnp.where(same & (line < lane), 1.0, 0.0), 0, keepdims=True)
    rank_col = jnp.sum(jnp.where(same & (lane < line), 1.0, 0.0), 1, keepdims=True)
    slot = iota((256, FIB), 0).astype(F32)
    into_slots = jnp.where(slot == sector_row * 4.0 + rank_row, 1.0, 0.0).astype(BF16)
    into_sectors = jnp.where(iota((SEC, FIB), 0).astype(F32) == sector_row, 1.0, 0.0)
    at_lane = (lane - 4 * lax.rem(me, 32)).astype(F32) == rank_col
    codes_out[...] = mxu(
        into_sectors.astype(BF16), jnp.where(at_lane, as_cols[:, 4:5] + 1.0, 0.0).astype(BF16)
    )

    for c in loads:
        c.wait()

    def fibres(i, carry):
        rows = pl.ds(pl.multiple_of(i * ROWS, ROWS), ROWS)
        points = iota((ROWS, 128), 1)
        first, last = points == 0, points == 127
        info = cols[rows, :]
        cond = jnp.broadcast_to(info[:, 0:1], (ROWS, 128))
        synapse, onset = info[:, 1:2], info[:, 2:3]
        state, onsets = [], []
        for half in range(2):
            at = slice(128 * half, 128 * half + 128)
            state.append([v_in[rows, at]] + [gates_in[q, rows, at] for q in range(3)])
            onsets.append(
                jnp.where((points + 128 * half).astype(F32) == synapse, onset, 1e9)
            )
        for k in range(SUBSTEPS):
            l0, l1, r0, r1 = neighbours(state[0][0], state[1][0], first, last)
            state = [
                membrane(k, *state[0], l0, r0, cond, onsets[0]),
                membrane(k, *state[1], l1, r1, cond, onsets[1]),
            ]
        for half in range(2):
            at = slice(128 * half, 128 * half + 128)
            v_new[rows, at] = state[half][0]
            for q in range(3):
                gates_new[q, rows, at] = state[half][1 + q]
        l0, l1, r0, r1 = neighbours(state[0][0], state[1][0], first, last)
        low = cond * (l0 + r0 - 2.0 * state[0][0])
        high = cond * (l1 + r1 - 2.0 * state[1][0])
        even = points % 32 < 16
        src[0, rows, :] = jnp.where(even, low, pltpu.roll(high, 16, 1))
        src[1, rows, :] = jnp.where(even, pltpu.roll(low, 112, 1), high)
        return carry

    lax.fori_loop(0, FIB // ROWS, fibres, 0)

    stores = [
        pltpu.make_async_copy(v_new, v_out, store_sem.at[0]),
        pltpu.make_async_copy(gates_new, gates_out, store_sem.at[1]),
    ]
    for c in stores:
        c.start()

    for c in range(2):
        s_hi, s_mid, s_lo = split3(src[c])
        placed[c] = mxu(into_slots, s_hi) + mxu(into_slots, s_mid) + mxu(into_slots, s_lo)

    pl.semaphore_wait(barrier, SEC + RADN - 2)

    def over_sectors(source, target, n, rows, over=over_partners):
        own = pl.ds(pl.multiple_of(me * rows, rows), rows)
        over(
            lambda d: pltpu.make_async_remote_copy(
                source.at[pl.ds(pl.multiple_of(d * rows, rows), rows)],
                target.at[own],
                send_sem.at[n],
                got_sem.at[n],
                device_id={"sec": d},
                device_id_type=MESH,
            ).start()
        )
        local = pltpu.make_async_copy(source.at[own], target.at[own], local_sem.at[n])
        local.start()
        return local

    def all_of(buffer, sem):
        pltpu.make_async_copy(buffer, buffer, sem).wait()

    most = pl.ds(0, SEC - 1)
    most4 = pl.ds(0, 4 * (SEC - 1))
    local_codes = over_sectors(codes_out, codes_in, 0, 1)
    local_fibres = [over_sectors(placed.at[0], got_fibres.at[0], 1, 4)]
    load_basis.wait()
    b_hi, b_lo = split2(basis[...].T)
    all_of(placed.at[0, most4], send_sem.at[1])
    local_fibres.append(over_sectors(placed.at[1], got_fibres.at[1], 2, 4))

    all_of(codes_in.at[most], got_sem.at[0])
    local_codes.wait()
    codes = jnp.concatenate(
        [
            jnp.sum(codes_in[0:32, :], 0, keepdims=True),
            jnp.sum(codes_in[32:64, :], 0, keepdims=True),
        ],
        1,
    )
    into_cells = jnp.where(iota((256, 256), 0).astype(F32) + 1.0 == codes, 1.0, 0.0).astype(BF16)

    lanes = iota((32, 128), 1)

    def deposit(c):
        all_of(got_fibres.at[c, most4], got_sem.at[1 + c])
        local_fibres[c].wait()
        x_hi, x_lo = split2(got_fibres[c])
        cells = mxu(into_cells, x_hi) + mxu(into_cells, x_lo)
        t = [cells[32 * a : 32 * a + 32] for a in range(8)]
        for step in (4, 2, 1):
            width = 16 * step
            late = lanes % (2 * width) >= width
            for a in range(8):
                if a // step % 2 == 0:
                    p, q = t[a], t[a + step]
                    t[a] = jnp.where(late, pltpu.roll(q, width, 1), p)
                    t[a + step] = jnp.where(late, q, pltpu.roll(p, 128 - width, 1))
        for q in range(8):
            slabs[c, q // 2 + 4 * (q % 2)] = t[q]
        for i in range(1, RADN):
            d = lax.rem(band + i, RADN)
            pltpu.make_async_remote_copy(
                slabs.at[c, d],
                field.at[c, band],
                send_sem.at[3 + c],
                got_sem.at[3 + c],
                device_id={"rad": d},
                device_id_type=MESH,
            ).start()
        local = pltpu.make_async_copy(slabs.at[c, band], field.at[c, band], local_sem.at[3 + c])
        local.start()
        return local

    def project(c, local):
        all_of(field.at[c, pl.ds(0, RADN - 1)], got_sem.at[3 + c])
        local.wait()
        f_hi, f_lo = split2(field[c].reshape(256, 128))
        projected[c] = mxu(b_hi, f_hi) + mxu(b_hi, f_lo) + mxu(b_lo, f_hi)
        return over_sectors(
            projected.at[c], got_all.at[c], 5 + c, 4, over_partners_in_order if c else over_partners
        )

    last_copies = []
    deposits = [deposit(c) for c in range(2)]
    for c in range(2):
        last_copies.append(project(c, deposits[c]))

    for c in stores:
        c.wait()
    all_of(codes_out.at[most], send_sem.at[0])
    for c in range(2):
        if c == 1:
            all_of(placed.at[c, most4], send_sem.at[1 + c])
        all_of(slabs.at[c, pl.ds(0, RADN - 1)], send_sem.at[3 + c])
    for c in range(2):
        all_of(got_all.at[c, most4], got_sem.at[5 + c])
        last_copies[c].wait()
        all_out[c] = got_all[c]
    for c in range(2):
        all_of(projected.at[c, most4], send_sem.at[5 + c])


def spectral_kernel(
    all_ref, table_hi, table_lo, spectrum_ref, v_hbm, gates_hbm, out_ref, v_out, gates_out, sem
):
    passed = [
        pltpu.make_async_copy(v_hbm, v_out, sem.at[0]),
        pltpu.make_async_copy(gates_hbm, gates_out, sem.at[1]),
    ]
    for c in passed:
        c.start()
    parts = []
    near = iota((64, 128), 1) < 64
    for j in range(4):
        first, second = (all_ref[c, pl.ds(j, 64, stride=4), :] for c in range(2))
        lower = jnp.where(near, first, pltpu.roll(second, 64, 1))
        upper = jnp.where(near, pltpu.roll(first, 64, 1), second)
        t = jnp.concatenate([lower, upper], 0).T
        for c in range(2):
            at = [64 * c + 16 * a for a in range(4)]
            parts.append(jnp.concatenate([t[i : i + 16] for i in at], 1))
    hi, lo = split2(jnp.concatenate(parts, 0))
    for tile in range(4):
        at = slice(128 * tile, 128 * tile + 128)
        scale = jnp.concatenate(
            [jnp.broadcast_to(spectrum_ref[j : j + 1, at], (32, 128)) for j in range(4)], 0
        )
        for part in range(2):
            to = slice(512 * part + 128 * tile, 512 * part + 128 * tile + 128)
            y = mxu(hi, table_hi[:, to]) + mxu(lo, table_hi[:, to]) + mxu(hi, table_lo[:, to])
            out_ref[pl.ds(2 * tile + part, 128, stride=8), :] = y * scale
    for c in passed:
        c.wait()


def azimuth_table():
    low, high, sector = np.meshgrid(np.arange(4), np.arange(2), np.arange(SEC), indexing="ij")
    azimuth = (sector * 8 + high * 4 + low).reshape(-1)
    phase = (azimuth[:, None] * np.arange(AZ)[None, :] % AZ) * (2.0 * math.pi / AZ)
    table = np.concatenate([np.cos(phase), -np.sin(phase)], 1) / math.sqrt(AZ)
    hi = table.astype(np.float32).astype(jnp.bfloat16)
    lo = (table - hi.astype(np.float64)).astype(np.float32).astype(jnp.bfloat16)
    return hi, lo


def per_device(
    voltage,
    gates,
    conductance,
    sector_map,
    cell_index,
    neuron,
    moment,
    synapse,
    basis,
    spectrum,
):
    any_space = pl.BlockSpec(memory_space=pl.ANY)
    vmem = pl.BlockSpec(memory_space=pltpu.VMEM)
    hbm = pl.BlockSpec(memory_space=pltpu.HBM)
    v_later, gates_later, everything = pl.pallas_call(
        exchange_kernel,
        out_shape=[
            jax.ShapeDtypeStruct((FIB, 256), F32),
            jax.ShapeDtypeStruct((3, FIB, 256), F32),
            jax.ShapeDtypeStruct((2, 256, 128), F32),
        ],
        in_specs=[hbm] * 9,
        out_specs=[any_space, any_space, vmem],
        scratch_shapes=[
            pltpu.VMEM((FIB, 256), F32),
            pltpu.VMEM((3, FIB, 256), F32),
            pltpu.VMEM((256, 256), F32),
            pltpu.VMEM((1, FIB), F32),
            pltpu.VMEM((1, FIB), jnp.int32),
            pltpu.VMEM((1, FIB), jnp.int32),
            pltpu.VMEM((1, FIB), jnp.int32),
            pltpu.VMEM((1, 512), jnp.int32),
            pltpu.VMEM((1, FIB), jnp.int32),
            pltpu.VMEM((FIB, 256), F32),
            pltpu.VMEM((3, FIB, 256), F32),
            pltpu.VMEM((FIB, 128), F32),
            pltpu.VMEM((2, FIB, 128), F32),
            pltpu.VMEM((SEC, 128), F32),
            pltpu.VMEM((SEC, 128), F32),
            pltpu.VMEM((2, 256, 128), F32),
            pltpu.VMEM((2, 256, 128), F32),
            pltpu.VMEM((2, 8, 32, 128), F32),
            pltpu.VMEM((2, 8, 32, 128), F32),
            pltpu.VMEM((2, 256, 128), F32),
            pltpu.VMEM((2, 256, 128), F32),
            pltpu.SemaphoreType.DMA((2,)),
            pltpu.SemaphoreType.DMA((6,)),
            pltpu.SemaphoreType.DMA,
            pltpu.SemaphoreType.DMA((2,)),
            pltpu.SemaphoreType.DMA((7,)),
            pltpu.SemaphoreType.DMA((7,)),
            pltpu.SemaphoreType.DMA((7,)),
        ],
        compiler_params=pltpu.CompilerParams(
            collective_id=0, has_side_effects=True, vmem_limit_bytes=32 << 20
        ),
        cost_estimate=pl.CostEstimate(
            flops=20_000_000_000, bytes_accessed=100_000_000, transcendentals=4_000_000
        ),
    )(
        *(
            pltpu.with_memory_space_constraint(a, pltpu.HBM)
            for a in (
                voltage,
                gates,
                basis,
                conductance.reshape(1, FIB),
                sector_map.reshape(1, FIB),
                cell_index.reshape(1, FIB),
                neuron.reshape(1, FIB),
                moment.reshape(1, 512),
                synapse.reshape(1, FIB),
            )
        )
    )
    table_hi, table_lo = azimuth_table()
    tiles, v_final, gates_final = pl.pallas_call(
        spectral_kernel,
        out_shape=[
            jax.ShapeDtypeStruct((1024, 128), F32),
            jax.ShapeDtypeStruct((FIB, 256), F32),
            jax.ShapeDtypeStruct((3, FIB, 256), F32),
        ],
        in_specs=[vmem] * 4 + [any_space] * 2,
        out_specs=[vmem, any_space, any_space],
        scratch_shapes=[pltpu.SemaphoreType.DMA((2,))],
        compiler_params=pltpu.CompilerParams(vmem_limit_bytes=32 << 20),
    )(
        everything,
        jnp.asarray(table_hi),
        jnp.asarray(table_lo),
        spectrum,
        v_later,
        gates_later,
    )
    potential = tiles.reshape(4, 32, 4, 2, 128).transpose(0, 1, 3, 2, 4).reshape(4, 32, 2, AZ)
    return v_final, gates_final, potential


def solution(mesh):
    placed = (
        P(("sec", "rad"), None),
        P(None, ("sec", "rad"), None),
        P(("sec", "rad")),
        P(("sec", "rad"), None),
        P(("sec", "rad")),
        P(("sec", "rad")),
        P(),
        P(("sec", "rad")),
        P(),
        P("sec", None),
    )
    return jax.shard_map(
        per_device,
        mesh=mesh,
        in_specs=placed,
        out_specs=(
            P(("sec", "rad"), None),
            P(None, ("sec", "rad"), None),
            P("sec", "rad", None, None),
        ),
        check_vma=False,
    )
```

```python
import functools
import math

import jax
import jax.numpy as jnp
import numpy as np
from jax import lax
from jax.experimental import pallas as pl
from jax.experimental.pallas import tpu as pltpu
from jax.sharding import PartitionSpec as P

F32 = jnp.float32
BF16 = jnp.bfloat16
MESH = pl.DeviceIdType.MESH

AZ = 512
SUBSTEPS = 10
SEC = 64
RADN = 8
FIB = 128
ROWS = 32


def split2(x):
    hi = x.astype(BF16)
    return hi, (x - hi.astype(F32)).astype(BF16)


def split3(x):
    hi = x.astype(BF16)
    rest = x - hi.astype(F32)
    mid = rest.astype(BF16)
    return hi, mid, (rest - mid.astype(F32)).astype(BF16)


def mxu(a, b, dims=((1,), (0,))):
    return lax.dot_general(a, b, (dims, ((), ())), preferred_element_type=F32)


def iota(shape, dim):
    return lax.broadcasted_iota(jnp.int32, shape, dim)


def inverse(x):
    return pltpu.reciprocal(x, approx=True)


def membrane(k, v, m, h, n, left, right, cond, onset):
    e80 = jnp.exp(jnp.minimum(v * (-100.0 / 80.0) + (-65.0 / 80.0), 10.0))
    e40 = e80 * e80
    e20 = e40 * e40
    e10 = e20 * e20
    close_m = jnp.exp(v * (-100.0 / 18.0) + (-65.0 / 18.0 + math.log(4.0)))
    open_h = 0.07 * e20
    close_n = 0.125 * e80
    open_m = jnp.maximum(v * 10.0 + 4.0 + jnp.log(1.0 + e10 * math.exp(2.5)), 0.0)
    open_n = jnp.maximum(v + 0.55 + 0.1 * jnp.log(1.0 + e10 * math.exp(1.0)), 0.0)
    close_h = inverse(1.0 + e10 * math.exp(3.0))
    gates = []
    for gate, opening, closing in (
        (m, open_m, close_m),
        (h, open_h, close_h),
        (n, open_n, close_n),
    ):
        rate = opening + closing
        steady = opening * inverse(rate)
        gates.append(steady + (gate - steady) * jnp.exp(rate * -0.005))
    nn = n * n
    ionic = (
        (m * m * m * h) * (0.6 * v - 0.3)
        + (nn * nn) * (0.18 * v + 0.1386)
        + (0.0015 * v + 0.000816)
    )
    stimulus = jnp.where(onset <= float(k), 0.04, 0.0)
    after = v + cond * (left + right - 2.0 * v) + (stimulus - ionic)
    return [after] + gates


def neighbours(low, high, first, last):
    up_low, up_high = pltpu.roll(low, 1, 1), pltpu.roll(high, 1, 1)
    down_low, down_high = pltpu.roll(low, 127, 1), pltpu.roll(high, 127, 1)
    return (
        jnp.where(first, low, up_low),
        jnp.where(first, up_low, up_high),
        jnp.where(last, down_high, down_low),
        jnp.where(last, high, down_high),
    )


def exchange_kernel(
    v_hbm,
    gates_hbm,
    basis_hbm,
    cond_hbm,
    sector_hbm,
    cell_hbm,
    neuron_hbm,
    moment_hbm,
    synapse_hbm,
    v_out,
    gates_out,
    all_out,
    v_in,
    gates_in,
    basis,
    cond_ref,
    sector_ref,
    cell_ref,
    neuron_ref,
    moment_ref,
    synapse_ref,
    v_new,
    gates_new,
    cols,
    src,
    codes_out,
    codes_in,
    placed,
    got_fibres,
    slabs,
    field,
    projected,
    got_all,
    load_sem,
    small_sem,
    basis_sem,
    store_sem,
    send_sem,
    local_sem,
    got_sem,
):
    me = lax.axis_index("sec")
    band = lax.axis_index("rad")

    barrier = pltpu.get_barrier_semaphore()

    y, z = me // 16, lax.rem(me, 16)

    def over_partners(act):
        def far(i, carry):
            away = 8 - (i + 1) // 2
            to_z = lax.rem(z + jnp.where(lax.rem(i, 2) == 1, away, 16 - away), 16)
            for to_y in (2, 1, 3, 0):
                act(lax.rem(y + to_y, 4) * 16 + to_z)
            return carry

        lax.fori_loop(0, 15, far, 0)
        for to_y in (2, 1, 3):
            act(lax.rem(y + to_y, 4) * 16 + z)

    def over_partners_in_order(act):
        def at_z(to_z, carry):
            for to_y in (2, 1, 3):
                act(lax.rem(y + to_y, 4) * 16 + to_z)

            @pl.when(to_z != z)
            def _():
                act(y * 16 + to_z)

            return carry

        lax.fori_loop(0, 16, at_z, 0)

    over_partners(
        lambda d: pl.semaphore_signal(
            barrier, inc=1, device_id={"sec": d}, device_id_type=MESH
        )
    )
    for i in range(1, RADN):
        pl.semaphore_signal(
            barrier, inc=1, device_id={"rad": lax.rem(band + i, RADN)}, device_id_type=MESH
        )

    loads = [
        pltpu.make_async_copy(v_hbm, v_in, load_sem.at[0]),
        pltpu.make_async_copy(gates_hbm, gates_in, load_sem.at[1]),
    ]
    for c in loads:
        c.start()
    small = [
        pltpu.make_async_copy(a, b, small_sem.at[i])
        for i, (a, b) in enumerate(
            [
                (cond_hbm, cond_ref),
                (sector_hbm, sector_ref),
                (cell_hbm, cell_ref),
                (neuron_hbm, neuron_ref),
                (moment_hbm, moment_ref),
                (synapse_hbm, synapse_ref),
            ]
        )
    ]
    for c in small:
        c.start()
    load_basis = pltpu.make_async_copy(basis_hbm, basis, basis_sem)
    load_basis.start()

    for c in small:
        c.wait()
    sector_row = sector_ref[...].astype(F32)
    stacked = jnp.concatenate(
        [
            cond_ref[...],
            synapse_ref[...].astype(F32),
            neuron_ref[...].astype(F32),
            sector_row,
            cell_ref[...].astype(F32),
            jnp.zeros((123, FIB), F32),
        ],
        0,
    )
    as_cols = stacked.T
    unit = iota((FIB, 512), 1).astype(F32)
    moments = moment_ref[...].astype(F32)
    onset_col = jnp.sum(jnp.where(as_cols[:, 2:3] == unit, moments, 0.0), 1, keepdims=True)
    line, lane = iota((FIB, FIB), 0), iota((FIB, FIB), 1)
    cols[...] = jnp.where(lane == 2, onset_col, as_cols)
    same = as_cols[:, 3:4] == sector_row
    rank_row = jnp.sum(jnp.where(same & (line < lane), 1.0, 0.0), 0, keepdims=True)
    rank_col = jnp.sum(jnp.where(same & (lane < line), 1.0, 0.0), 1, keepdims=True)
    slot = iota((256, FIB), 0).astype(F32)
    into_slots = jnp.where(slot == sector_row * 4.0 + rank_row, 1.0, 0.0).astype(BF16)
    into_sectors = jnp.where(iota((SEC, FIB), 0).astype(F32) == sector_row, 1.0, 0.0)
    at_lane = (lane - 4 * lax.rem(me, 32)).astype(F32) == rank_col
    codes_out[...] = mxu(
        into_sectors.astype(BF16), jnp.where(at_lane, as_cols[:, 4:5] + 1.0, 0.0).astype(BF16)
    )

    for c in loads:
        c.wait()

    def fibres(i, carry):
        rows = pl.ds(pl.multiple_of(i * ROWS, ROWS), ROWS)
        points = iota((ROWS, 128), 1)
        first, last = points == 0, points == 127
        info = cols[rows, :]
        cond = jnp.broadcast_to(info[:, 0:1], (ROWS, 128))
        synapse, onset = info[:, 1:2], info[:, 2:3]
        state, onsets = [], []
        for half in range(2):
            at = slice(128 * half, 128 * half + 128)
            state.append([v_in[rows, at]] + [gates_in[q, rows, at] for q in range(3)])
            onsets.append(
                jnp.where((points + 128 * half).astype(F32) == synapse, onset, 1e9)
            )
        for k in range(SUBSTEPS):
            l0, l1, r0, r1 = neighbours(state[0][0], state[1][0], first, last)
            state = [
                membrane(k, *state[0], l0, r0, cond, onsets[0]),
                membrane(k, *state[1], l1, r1, cond, onsets[1]),
            ]
        for half in range(2):
            at = slice(128 * half, 128 * half + 128)
            v_new[rows, at] = state[half][0]
            for q in range(3):
                gates_new[q, rows, at] = state[half][1 + q]
        l0, l1, r0, r1 = neighbours(state[0][0], state[1][0], first, last)
        low = cond * (l0 + r0 - 2.0 * state[0][0])
        high = cond * (l1 + r1 - 2.0 * state[1][0])
        even = points % 32 < 16
        src[0, rows, :] = jnp.where(even, low, pltpu.roll(high, 16, 1))
        src[1, rows, :] = jnp.where(even, pltpu.roll(low, 112, 1), high)
        return carry

    lax.fori_loop(0, FIB // ROWS, fibres, 0)

    stores = [
        pltpu.make_async_copy(v_new, v_out, store_sem.at[0]),
        pltpu.make_async_copy(gates_new, gates_out, store_sem.at[1]),
    ]
    for c in stores:
        c.start()

    for c in range(2):
        s_hi, s_mid, s_lo = split3(src[c])
        placed[c] = mxu(into_slots, s_hi) + mxu(into_slots, s_mid) + mxu(into_slots, s_lo)

    pl.semaphore_wait(barrier, SEC + RADN - 2)

    def over_sectors(source, target, n, rows, over=over_partners):
        own = pl.ds(pl.multiple_of(me * rows, rows), rows)
        over(
            lambda d: pltpu.make_async_remote_copy(
                source.at[pl.ds(pl.multiple_of(d * rows, rows), rows)],
                target.at[own],
                send_sem.at[n],
                got_sem.at[n],
                device_id={"sec": d},
                device_id_type=MESH,
            ).start()
        )
        local = pltpu.make_async_copy(source.at[own], target.at[own], local_sem.at[n])
        local.start()
        return local

    def all_of(buffer, sem):
        pltpu.make_async_copy(buffer, buffer, sem).wait()

    most = pl.ds(0, SEC - 1)
    most4 = pl.ds(0, 4 * (SEC - 1))
    local_codes = over_sectors(codes_out, codes_in, 0, 1)
    local_fibres = [over_sectors(placed.at[0], got_fibres.at[0], 1, 4)]
    load_basis.wait()
    b_hi, b_lo = split2(basis[...].T)
    all_of(placed.at[0, most4], send_sem.at[1])
    local_fibres.append(over_sectors(placed.at[1], got_fibres.at[1], 2, 4))

    all_of(codes_in.at[most], got_sem.at[0])
    local_codes.wait()
    codes = jnp.concatenate(
        [
            jnp.sum(codes_in[0:32, :], 0, keepdims=True),
            jnp.sum(codes_in[32:64, :], 0, keepdims=True),
        ],
        1,
    )
    into_cells = jnp.where(iota((256, 256), 0).astype(F32) + 1.0 == codes, 1.0, 0.0).astype(BF16)

    lanes = iota((32, 128), 1)

    def deposit(c):
        all_of(got_fibres.at[c, most4], got_sem.at[1 + c])
        local_fibres[c].wait()
        x_hi, x_lo = split2(got_fibres[c])
        cells = mxu(into_cells, x_hi) + mxu(into_cells, x_lo)
        t = [cells[32 * a : 32 * a + 32] for a in range(8)]
        for step in (4, 2, 1):
            width = 16 * step
            late = lanes % (2 * width) >= width
            for a in range(8):
                if a // step % 2 == 0:
                    p, q = t[a], t[a + step]
                    t[a] = jnp.where(late, pltpu.roll(q, width, 1), p)
                    t[a + step] = jnp.where(late, q, pltpu.roll(p, 128 - width, 1))
        for q in range(8):
            slabs[c, q // 2 + 4 * (q % 2)] = t[q]
        for i in (4, 3, 5, 2, 6, 1, 7):
            d = lax.rem(band + i, RADN)
            pltpu.make_async_remote_copy(
                slabs.at[c, d],
                field.at[c, band],
                send_sem.at[3 + c],
                got_sem.at[3 + c],
                device_id={"rad": d},
                device_id_type=MESH,
            ).start()
        local = pltpu.make_async_copy(slabs.at[c, band], field.at[c, band], local_sem.at[3 + c])
        local.start()
        return local

    def project(c, local):
        all_of(field.at[c, pl.ds(0, RADN - 1)], got_sem.at[3 + c])
        local.wait()
        f_hi, f_lo = split2(field[c].reshape(256, 128))
        projected[c] = mxu(b_hi, f_hi) + mxu(b_hi, f_lo) + mxu(b_lo, f_hi)
        return over_sectors(
            projected.at[c], got_all.at[c], 5 + c, 4, over_partners_in_order if c else over_partners
        )

    last_copies = []
    deposits = [deposit(c) for c in range(2)]
    for c in range(2):
        last_copies.append(project(c, deposits[c]))

    for c in stores:
        c.wait()
    all_of(codes_out.at[most], send_sem.at[0])
    for c in range(2):
        if c == 1:
            all_of(placed.at[c, most4], send_sem.at[1 + c])
        all_of(slabs.at[c, pl.ds(0, RADN - 1)], send_sem.at[3 + c])
    for c in range(2):
        all_of(got_all.at[c, most4], got_sem.at[5 + c])
        last_copies[c].wait()
        all_out[c] = got_all[c]
    for c in range(2):
        all_of(projected.at[c, most4], send_sem.at[5 + c])


def spectral_kernel(
    all_ref, table_hi, table_lo, spectrum_ref, v_hbm, gates_hbm, out_ref, v_out, gates_out, sem
):
    passed = [
        pltpu.make_async_copy(v_hbm, v_out, sem.at[0]),
        pltpu.make_async_copy(gates_hbm, gates_out, sem.at[1]),
    ]
    for c in passed:
        c.start()
    parts = []
    near = iota((64, 128), 1) < 64
    for j in range(4):
        first, second = (all_ref[c, pl.ds(j, 64, stride=4), :] for c in range(2))
        lower = jnp.where(near, first, pltpu.roll(second, 64, 1))
        upper = jnp.where(near, pltpu.roll(first, 64, 1), second)
        t = jnp.concatenate([lower, upper], 0).T
        for c in range(2):
            at = [64 * c + 16 * a for a in range(4)]
            parts.append(jnp.concatenate([t[i : i + 16] for i in at], 1))
    hi, lo = split2(jnp.concatenate(parts, 0))
    for pair in range(2):
        at = slice(256 * pair, 256 * pair + 256)
        scale = jnp.concatenate(
            [jnp.broadcast_to(spectrum_ref[j : j + 1, at], (32, 256)) for j in range(4)], 0
        )
        for part in range(2):
            to = slice(512 * part + 256 * pair, 512 * part + 256 * pair + 256)
            y = mxu(hi, table_hi[:, to]) + mxu(lo, table_hi[:, to]) + mxu(hi, table_lo[:, to])
            y = y * scale
            for tile in range(2):
                out_ref[pl.ds(4 * pair + 2 * tile + part, 128, stride=8), :] = y[
                    :, 128 * tile : 128 * tile + 128
                ]
    for c in passed:
        c.wait()


def azimuth_table():
    low, high, sector = np.meshgrid(np.arange(4), np.arange(2), np.arange(SEC), indexing="ij")
    azimuth = (sector * 8 + high * 4 + low).reshape(-1)
    phase = (azimuth[:, None] * np.arange(AZ)[None, :] % AZ) * (2.0 * math.pi / AZ)
    table = np.concatenate([np.cos(phase), -np.sin(phase)], 1) / math.sqrt(AZ)
    hi = table.astype(np.float32).astype(jnp.bfloat16)
    lo = (table - hi.astype(np.float64)).astype(np.float32).astype(jnp.bfloat16)
    return hi, lo


def per_device(
    voltage,
    gates,
    conductance,
    sector_map,
    cell_index,
    neuron,
    moment,
    synapse,
    basis,
    spectrum,
):
    any_space = pl.BlockSpec(memory_space=pl.ANY)
    vmem = pl.BlockSpec(memory_space=pltpu.VMEM)
    hbm = pl.BlockSpec(memory_space=pltpu.HBM)
    v_later, gates_later, everything = pl.pallas_call(
        exchange_kernel,
        out_shape=[
            jax.ShapeDtypeStruct((FIB, 256), F32),
            jax.ShapeDtypeStruct((3, FIB, 256), F32),
            jax.ShapeDtypeStruct((2, 256, 128), F32),
        ],
        in_specs=[hbm] * 9,
        out_specs=[any_space, any_space, vmem],
        scratch_shapes=[
            pltpu.VMEM((FIB, 256), F32),
            pltpu.VMEM((3, FIB, 256), F32),
            pltpu.VMEM((256, 256), F32),
            pltpu.VMEM((1, FIB), F32),
            pltpu.VMEM((1, FIB), jnp.int32),
            pltpu.VMEM((1, FIB), jnp.int32),
            pltpu.VMEM((1, FIB), jnp.int32),
            pltpu.VMEM((1, 512), jnp.int32),
            pltpu.VMEM((1, FIB), jnp.int32),
            pltpu.VMEM((FIB, 256), F32),
            pltpu.VMEM((3, FIB, 256), F32),
            pltpu.VMEM((FIB, 128), F32),
            pltpu.VMEM((2, FIB, 128), F32),
            pltpu.VMEM((SEC, 128), F32),
            pltpu.VMEM((SEC, 128), F32),
            pltpu.VMEM((2, 256, 128), F32),
            pltpu.VMEM((2, 256, 128), F32),
            pltpu.VMEM((2, 8, 32, 128), F32),
            pltpu.VMEM((2, 8, 32, 128), F32),
            pltpu.VMEM((2, 256, 128), F32),
            pltpu.VMEM((2, 256, 128), F32),
            pltpu.SemaphoreType.DMA((2,)),
            pltpu.SemaphoreType.DMA((6,)),
            pltpu.SemaphoreType.DMA,
            pltpu.SemaphoreType.DMA((2,)),
            pltpu.SemaphoreType.DMA((7,)),
            pltpu.SemaphoreType.DMA((7,)),
            pltpu.SemaphoreType.DMA((7,)),
        ],
        compiler_params=pltpu.CompilerParams(
            collective_id=0, has_side_effects=True, vmem_limit_bytes=32 << 20
        ),
        cost_estimate=pl.CostEstimate(
            flops=20_000_000_000, bytes_accessed=100_000_000, transcendentals=4_000_000
        ),
    )(
        *(
            pltpu.with_memory_space_constraint(a, pltpu.HBM)
            for a in (
                voltage,
                gates,
                basis,
                conductance.reshape(1, FIB),
                sector_map.reshape(1, FIB),
                cell_index.reshape(1, FIB),
                neuron.reshape(1, FIB),
                moment.reshape(1, 512),
                synapse.reshape(1, FIB),
            )
        )
    )
    table_hi, table_lo = azimuth_table()
    tiles, v_final, gates_final = pl.pallas_call(
        spectral_kernel,
        out_shape=[
            jax.ShapeDtypeStruct((1024, 128), F32),
            jax.ShapeDtypeStruct((FIB, 256), F32),
            jax.ShapeDtypeStruct((3, FIB, 256), F32),
        ],
        in_specs=[vmem] * 4 + [any_space] * 2,
        out_specs=[vmem, any_space, any_space],
        scratch_shapes=[pltpu.SemaphoreType.DMA((2,))],
        compiler_params=pltpu.CompilerParams(vmem_limit_bytes=32 << 20),
    )(
        everything,
        jnp.asarray(table_hi),
        jnp.asarray(table_lo),
        spectrum,
        v_later,
        gates_later,
    )
    potential = tiles.reshape(4, 32, 4, 2, 128).transpose(0, 1, 3, 2, 4).reshape(4, 32, 2, AZ)
    return v_final, gates_final, potential


def solution(mesh):
    placed = (
        P(("sec", "rad"), None),
        P(None, ("sec", "rad"), None),
        P(("sec", "rad")),
        P(("sec", "rad"), None),
        P(("sec", "rad")),
        P(("sec", "rad")),
        P(),
        P(("sec", "rad")),
        P(),
        P("sec", None),
    )
    return jax.shard_map(
        per_device,
        mesh=mesh,
        in_specs=placed,
        out_specs=(
            P(("sec", "rad"), None),
            P(None, ("sec", "rad"), None),
            P("sec", "rad", None, None),
        ),
        check_vma=False,
    )
```

```python
import functools
import math

import jax
import jax.numpy as jnp
import numpy as np
from jax import lax
from jax.experimental import pallas as pl
from jax.experimental.pallas import tpu as pltpu
from jax.sharding import PartitionSpec as P

F32 = jnp.float32
BF16 = jnp.bfloat16
MESH = pl.DeviceIdType.MESH

AZ = 512
SUBSTEPS = 10
SEC = 64
RADN = 8
FIB = 128
ROWS = 32


def split2(x):
    hi = x.astype(BF16)
    return hi, (x - hi.astype(F32)).astype(BF16)


def split3(x):
    hi = x.astype(BF16)
    rest = x - hi.astype(F32)
    mid = rest.astype(BF16)
    return hi, mid, (rest - mid.astype(F32)).astype(BF16)


def mxu(a, b, dims=((1,), (0,))):
    return lax.dot_general(a, b, (dims, ((), ())), preferred_element_type=F32)


def iota(shape, dim):
    return lax.broadcasted_iota(jnp.int32, shape, dim)


def inverse(x):
    return pltpu.reciprocal(x, approx=True)


def membrane(k, v, m, h, n, left, right, cond, onset):
    e80 = jnp.exp(jnp.minimum(v * (-100.0 / 80.0) + (-65.0 / 80.0), 10.0))
    e40 = e80 * e80
    e20 = e40 * e40
    e10 = e20 * e20
    close_m = jnp.exp(v * (-100.0 / 18.0) + (-65.0 / 18.0 + math.log(4.0)))
    open_h = 0.07 * e20
    close_n = 0.125 * e80
    open_m = jnp.maximum(v * 10.0 + 4.0 + jnp.log(1.0 + e10 * math.exp(2.5)), 0.0)
    open_n = jnp.maximum(v + 0.55 + 0.1 * jnp.log(1.0 + e10 * math.exp(1.0)), 0.0)
    close_h = inverse(1.0 + e10 * math.exp(3.0))
    gates = []
    for gate, opening, closing in (
        (m, open_m, close_m),
        (h, open_h, close_h),
        (n, open_n, close_n),
    ):
        rate = opening + closing
        steady = opening * inverse(rate)
        gates.append(steady + (gate - steady) * jnp.exp(rate * -0.005))
    nn = n * n
    ionic = (
        (m * m * m * h) * (0.6 * v - 0.3)
        + (nn * nn) * (0.18 * v + 0.1386)
        + (0.0015 * v + 0.000816)
    )
    stimulus = jnp.where(onset <= float(k), 0.04, 0.0)
    after = v + cond * (left + right - 2.0 * v) + (stimulus - ionic)
    return [after] + gates


def neighbours(low, high, first, last):
    up_low, up_high = pltpu.roll(low, 1, 1), pltpu.roll(high, 1, 1)
    down_low, down_high = pltpu.roll(low, 127, 1), pltpu.roll(high, 127, 1)
    return (
        jnp.where(first, low, up_low),
        jnp.where(first, up_low, up_high),
        jnp.where(last, down_high, down_low),
        jnp.where(last, high, down_high),
    )


def exchange_kernel(
    v_hbm,
    gates_hbm,
    basis_hbm,
    cond_hbm,
    sector_hbm,
    cell_hbm,
    neuron_hbm,
    moment_hbm,
    synapse_hbm,
    v_out,
    gates_out,
    all_out,
    v_in,
    gates_in,
    basis,
    cond_ref,
    sector_ref,
    cell_ref,
    neuron_ref,
    moment_ref,
    synapse_ref,
    v_new,
    gates_new,
    cols,
    src,
    codes_out,
    codes_in,
    placed,
    got_fibres,
    slabs,
    field,
    projected,
    got_all,
    load_sem,
    small_sem,
    basis_sem,
    store_sem,
    send_sem,
    local_sem,
    got_sem,
):
    me = lax.axis_index("sec")
    band = lax.axis_index("rad")

    barrier = pltpu.get_barrier_semaphore()

    y, z = me // 16, lax.rem(me, 16)

    def over_partners(act):
        def far(i, carry):
            away = 8 - (i + 1) // 2
            to_z = lax.rem(z + jnp.where(lax.rem(i, 2) == 1, away, 16 - away), 16)
            for to_y in (2, 1, 3, 0):
                act(lax.rem(y + to_y, 4) * 16 + to_z)
            return carry

        lax.fori_loop(0, 15, far, 0)
        for to_y in (2, 1, 3):
            act(lax.rem(y + to_y, 4) * 16 + z)

    def over_partners_in_order(act):
        def at_z(to_z, carry):
            for to_y in (2, 1, 3):
                act(lax.rem(y + to_y, 4) * 16 + to_z)

            @pl.when(to_z != z)
            def _():
                act(y * 16 + to_z)

            return carry

        lax.fori_loop(0, 16, at_z, 0)

    over_partners(
        lambda d: pl.semaphore_signal(
            barrier, inc=1, device_id={"sec": d}, device_id_type=MESH
        )
    )
    for i in range(1, RADN):
        pl.semaphore_signal(
            barrier, inc=1, device_id={"rad": lax.rem(band + i, RADN)}, device_id_type=MESH
        )

    loads = [
        pltpu.make_async_copy(v_hbm, v_in, load_sem.at[0]),
        pltpu.make_async_copy(gates_hbm, gates_in, load_sem.at[1]),
    ]
    for c in loads:
        c.start()
    small = [
        pltpu.make_async_copy(a, b, small_sem.at[i])
        for i, (a, b) in enumerate(
            [
                (cond_hbm, cond_ref),
                (sector_hbm, sector_ref),
                (cell_hbm, cell_ref),
                (neuron_hbm, neuron_ref),
                (moment_hbm, moment_ref),
                (synapse_hbm, synapse_ref),
            ]
        )
    ]
    for c in small:
        c.start()
    load_basis = pltpu.make_async_copy(basis_hbm, basis, basis_sem)
    load_basis.start()

    for c in small:
        c.wait()
    sector_row = sector_ref[...].astype(F32)
    stacked = jnp.concatenate(
        [
            cond_ref[...],
            synapse_ref[...].astype(F32),
            neuron_ref[...].astype(F32),
            sector_row,
            cell_ref[...].astype(F32),
            jnp.zeros((123, FIB), F32),
        ],
        0,
    )
    as_cols = stacked.T
    unit = iota((FIB, 512), 1).astype(F32)
    moments = moment_ref[...].astype(F32)
    onset_col = jnp.sum(jnp.where(as_cols[:, 2:3] == unit, moments, 0.0), 1, keepdims=True)
    line, lane = iota((FIB, FIB), 0), iota((FIB, FIB), 1)
    cols[...] = jnp.where(lane == 2, onset_col, as_cols)
    same = as_cols[:, 3:4] == sector_row
    rank_row = jnp.sum(jnp.where(same & (line < lane), 1.0, 0.0), 0, keepdims=True)
    rank_col = jnp.sum(jnp.where(same & (lane < line), 1.0, 0.0), 1, keepdims=True)
    slot = iota((256, FIB), 0).astype(F32)
    into_slots = jnp.where(slot == sector_row * 4.0 + rank_row, 1.0, 0.0).astype(BF16)
    into_sectors = jnp.where(iota((SEC, FIB), 0).astype(F32) == sector_row, 1.0, 0.0)
    at_lane = (lane - 4 * lax.rem(me, 32)).astype(F32) == rank_col
    codes_out[...] = mxu(
        into_sectors.astype(BF16), jnp.where(at_lane, as_cols[:, 4:5] + 1.0, 0.0).astype(BF16)
    )

    for c in loads:
        c.wait()

    def fibres(i, carry):
        rows = pl.ds(pl.multiple_of(i * ROWS, ROWS), ROWS)
        points = iota((ROWS, 128), 1)
        first, last = points == 0, points == 127
        info = cols[rows, :]
        cond = jnp.broadcast_to(info[:, 0:1], (ROWS, 128))
        synapse, onset = info[:, 1:2], info[:, 2:3]
        state, onsets = [], []
        for half in range(2):
            at = slice(128 * half, 128 * half + 128)
            state.append([v_in[rows, at]] + [gates_in[q, rows, at] for q in range(3)])
            onsets.append(
                jnp.where((points + 128 * half).astype(F32) == synapse, onset, 1e9)
            )
        for k in range(SUBSTEPS):
            l0, l1, r0, r1 = neighbours(state[0][0], state[1][0], first, last)
            state = [
                membrane(k, *state[0], l0, r0, cond, onsets[0]),
                membrane(k, *state[1], l1, r1, cond, onsets[1]),
            ]
        for half in range(2):
            at = slice(128 * half, 128 * half + 128)
            v_new[rows, at] = state[half][0]
            for q in range(3):
                gates_new[q, rows, at] = state[half][1 + q]
        l0, l1, r0, r1 = neighbours(state[0][0], state[1][0], first, last)
        low = cond * (l0 + r0 - 2.0 * state[0][0])
        high = cond * (l1 + r1 - 2.0 * state[1][0])
        even = points % 32 < 16
        src[0, rows, :] = jnp.where(even, low, pltpu.roll(high, 16, 1))
        src[1, rows, :] = jnp.where(even, pltpu.roll(low, 112, 1), high)
        return carry

    lax.fori_loop(0, FIB // ROWS, fibres, 0)

    stores = [
        pltpu.make_async_copy(v_new, v_out, store_sem.at[0]),
        pltpu.make_async_copy(gates_new, gates_out, store_sem.at[1]),
    ]
    for c in stores:
        c.start()

    for c in range(2):
        s_hi, s_mid, s_lo = split3(src[c])
        placed[c] = mxu(into_slots, s_hi) + mxu(into_slots, s_mid) + mxu(into_slots, s_lo)

    pl.semaphore_wait(barrier, SEC + RADN - 2)

    def over_sectors(source, target, n, rows, over=over_partners):
        own = pl.ds(pl.multiple_of(me * rows, rows), rows)
        over(
            lambda d: pltpu.make_async_remote_copy(
                source.at[pl.ds(pl.multiple_of(d * rows, rows), rows)],
                target.at[own],
                send_sem.at[n],
                got_sem.at[n],
                device_id={"sec": d},
                device_id_type=MESH,
            ).start()
        )
        local = pltpu.make_async_copy(source.at[own], target.at[own], local_sem.at[n])
        local.start()
        return local

    def all_of(buffer, sem):
        pltpu.make_async_copy(buffer, buffer, sem).wait()

    most = pl.ds(0, SEC - 1)
    most4 = pl.ds(0, 4 * (SEC - 1))
    local_codes = over_sectors(codes_out, codes_in, 0, 1)
    local_fibres = [over_sectors(placed.at[0], got_fibres.at[0], 1, 4)]
    load_basis.wait()
    b_hi, b_lo = split2(basis[...].T)
    all_of(placed.at[0, most4], send_sem.at[1])
    local_fibres.append(over_sectors(placed.at[1], got_fibres.at[1], 2, 4))

    all_of(codes_in.at[most], got_sem.at[0])
    local_codes.wait()
    codes = jnp.concatenate(
        [
            jnp.sum(codes_in[0:32, :], 0, keepdims=True),
            jnp.sum(codes_in[32:64, :], 0, keepdims=True),
        ],
        1,
    )
    into_cells = jnp.where(iota((256, 256), 0).astype(F32) + 1.0 == codes, 1.0, 0.0).astype(BF16)

    lanes = iota((32, 128), 1)

    def deposit(c):
        all_of(got_fibres.at[c, most4], got_sem.at[1 + c])
        local_fibres[c].wait()
        x_hi, x_lo = split2(got_fibres[c])
        cells = mxu(into_cells, x_hi) + mxu(into_cells, x_lo)
        t = [cells[32 * a : 32 * a + 32] for a in range(8)]
        for step in (4, 2, 1):
            width = 16 * step
            late = lanes % (2 * width) >= width
            for a in range(8):
                if a // step % 2 == 0:
                    p, q = t[a], t[a + step]
                    t[a] = jnp.where(late, pltpu.roll(q, width, 1), p)
                    t[a + step] = jnp.where(late, q, pltpu.roll(p, 128 - width, 1))
        for q in range(8):
            slabs[c, q // 2 + 4 * (q % 2)] = t[q]
        for i in (4, 3, 5, 2, 6, 1, 7):
            d = lax.rem(band + i, RADN)
            pltpu.make_async_remote_copy(
                slabs.at[c, d],
                field.at[c, band],
                send_sem.at[3 + c],
                got_sem.at[3 + c],
                device_id={"rad": d},
                device_id_type=MESH,
            ).start()
        local = pltpu.make_async_copy(slabs.at[c, band], field.at[c, band], local_sem.at[3 + c])
        local.start()
        return local

    def project(c, local):
        all_of(field.at[c, pl.ds(0, RADN - 1)], got_sem.at[3 + c])
        local.wait()
        f_hi, f_lo = split2(field[c].reshape(256, 128))
        projected[c] = mxu(b_hi, f_hi) + mxu(b_hi, f_lo) + mxu(b_lo, f_hi)
        return over_sectors(
            projected.at[c], got_all.at[c], 5 + c, 4, over_partners_in_order if c else over_partners
        )

    last_copies = []
    deposits = [deposit(c) for c in range(2)]
    for c in range(2):
        last_copies.append(project(c, deposits[c]))

    for c in stores:
        c.wait()
    all_of(codes_out.at[most], send_sem.at[0])
    for c in range(2):
        if c == 1:
            all_of(placed.at[c, most4], send_sem.at[1 + c])
        all_of(slabs.at[c, pl.ds(0, RADN - 1)], send_sem.at[3 + c])
    for c in range(2):
        all_of(got_all.at[c, most4], got_sem.at[5 + c])
        last_copies[c].wait()
        all_out[c] = got_all[c]
    for c in range(2):
        all_of(projected.at[c, most4], send_sem.at[5 + c])


def spectral_kernel(
    all_ref, table_hi, table_lo, spectrum_ref, v_hbm, gates_hbm, out_hbm, v_out, gates_out, tiles, sem
):
    passed = [
        pltpu.make_async_copy(v_hbm, v_out, sem.at[0]),
        pltpu.make_async_copy(gates_hbm, gates_out, sem.at[1]),
    ]
    for c in passed:
        c.start()
    parts = []
    near = iota((64, 128), 1) < 64
    for j in range(4):
        first, second = (all_ref[c, pl.ds(j, 64, stride=4), :] for c in range(2))
        lower = jnp.where(near, first, pltpu.roll(second, 64, 1))
        upper = jnp.where(near, pltpu.roll(first, 64, 1), second)
        t = jnp.concatenate([lower, upper], 0).T
        for c in range(2):
            at = [64 * c + 16 * a for a in range(4)]
            parts.append(jnp.concatenate([t[i : i + 16] for i in at], 1))
    for half in range(2):
        hi, lo = split2(jnp.concatenate(parts[4 * half : 4 * half + 4], 0))
        for pair in range(2):
            at = slice(256 * pair, 256 * pair + 256)
            scale = jnp.concatenate(
                [
                    jnp.broadcast_to(spectrum_ref[j : j + 1, at], (32, 256))
                    for j in (2 * half, 2 * half + 1)
                ],
                0,
            )
            for part in range(2):
                to = slice(512 * part + 256 * pair, 512 * part + 256 * pair + 256)
                y = mxu(hi, table_hi[:, to]) + mxu(lo, table_hi[:, to]) + mxu(hi, table_lo[:, to])
                y = y * scale
                for tile in range(2):
                    start = 512 * half + 4 * pair + 2 * tile + part
                    tiles[pl.ds(start, 64, stride=8), :] = y[:, 128 * tile : 128 * tile + 128]
        rows = pl.ds(512 * half, 512)
        passed.append(pltpu.make_async_copy(tiles.at[rows], out_hbm.at[rows], sem.at[2 + half]))
        passed[-1].start()
    for c in passed:
        c.wait()


def azimuth_table():
    low, high, sector = np.meshgrid(np.arange(4), np.arange(2), np.arange(SEC), indexing="ij")
    azimuth = (sector * 8 + high * 4 + low).reshape(-1)
    phase = (azimuth[:, None] * np.arange(AZ)[None, :] % AZ) * (2.0 * math.pi / AZ)
    table = np.concatenate([np.cos(phase), -np.sin(phase)], 1) / math.sqrt(AZ)
    hi = table.astype(np.float32).astype(jnp.bfloat16)
    lo = (table - hi.astype(np.float64)).astype(np.float32).astype(jnp.bfloat16)
    return hi, lo


def per_device(
    voltage,
    gates,
    conductance,
    sector_map,
    cell_index,
    neuron,
    moment,
    synapse,
    basis,
    spectrum,
):
    any_space = pl.BlockSpec(memory_space=pl.ANY)
    vmem = pl.BlockSpec(memory_space=pltpu.VMEM)
    hbm = pl.BlockSpec(memory_space=pltpu.HBM)
    v_later, gates_later, everything = pl.pallas_call(
        exchange_kernel,
        out_shape=[
            jax.ShapeDtypeStruct((FIB, 256), F32),
            jax.ShapeDtypeStruct((3, FIB, 256), F32),
            jax.ShapeDtypeStruct((2, 256, 128), F32),
        ],
        in_specs=[hbm] * 9,
        out_specs=[any_space, any_space, vmem],
        scratch_shapes=[
            pltpu.VMEM((FIB, 256), F32),
            pltpu.VMEM((3, FIB, 256), F32),
            pltpu.VMEM((256, 256), F32),
            pltpu.VMEM((1, FIB), F32),
            pltpu.VMEM((1, FIB), jnp.int32),
            pltpu.VMEM((1, FIB), jnp.int32),
            pltpu.VMEM((1, FIB), jnp.int32),
            pltpu.VMEM((1, 512), jnp.int32),
            pltpu.VMEM((1, FIB), jnp.int32),
            pltpu.VMEM((FIB, 256), F32),
            pltpu.VMEM((3, FIB, 256), F32),
            pltpu.VMEM((FIB, 128), F32),
            pltpu.VMEM((2, FIB, 128), F32),
            pltpu.VMEM((SEC, 128), F32),
            pltpu.VMEM((SEC, 128), F32),
            pltpu.VMEM((2, 256, 128), F32),
            pltpu.VMEM((2, 256, 128), F32),
            pltpu.VMEM((2, 8, 32, 128), F32),
            pltpu.VMEM((2, 8, 32, 128), F32),
            pltpu.VMEM((2, 256, 128), F32),
            pltpu.VMEM((2, 256, 128), F32),
            pltpu.SemaphoreType.DMA((2,)),
            pltpu.SemaphoreType.DMA((6,)),
            pltpu.SemaphoreType.DMA,
            pltpu.SemaphoreType.DMA((2,)),
            pltpu.SemaphoreType.DMA((7,)),
            pltpu.SemaphoreType.DMA((7,)),
            pltpu.SemaphoreType.DMA((7,)),
        ],
        compiler_params=pltpu.CompilerParams(
            collective_id=0, has_side_effects=True, vmem_limit_bytes=32 << 20
        ),
        cost_estimate=pl.CostEstimate(
            flops=20_000_000_000, bytes_accessed=100_000_000, transcendentals=4_000_000
        ),
    )(
        *(
            pltpu.with_memory_space_constraint(a, pltpu.HBM)
            for a in (
                voltage,
                gates,
                basis,
                conductance.reshape(1, FIB),
                sector_map.reshape(1, FIB),
                cell_index.reshape(1, FIB),
                neuron.reshape(1, FIB),
                moment.reshape(1, 512),
                synapse.reshape(1, FIB),
            )
        )
    )
    table_hi, table_lo = azimuth_table()
    tiles, v_final, gates_final = pl.pallas_call(
        spectral_kernel,
        out_shape=[
            jax.ShapeDtypeStruct((1024, 128), F32),
            jax.ShapeDtypeStruct((FIB, 256), F32),
            jax.ShapeDtypeStruct((3, FIB, 256), F32),
        ],
        in_specs=[vmem] * 4 + [any_space] * 2,
        out_specs=[any_space] * 3,
        scratch_shapes=[pltpu.VMEM((1024, 128), F32), pltpu.SemaphoreType.DMA((4,))],
        compiler_params=pltpu.CompilerParams(vmem_limit_bytes=32 << 20),
    )(
        everything,
        jnp.asarray(table_hi),
        jnp.asarray(table_lo),
        spectrum,
        v_later,
        gates_later,
    )
    potential = tiles.reshape(4, 32, 4, 2, 128).transpose(0, 1, 3, 2, 4).reshape(4, 32, 2, AZ)
    return v_final, gates_final, potential


def solution(mesh):
    placed = (
        P(("sec", "rad"), None),
        P(None, ("sec", "rad"), None),
        P(("sec", "rad")),
        P(("sec", "rad"), None),
        P(("sec", "rad")),
        P(("sec", "rad")),
        P(),
        P(("sec", "rad")),
        P(),
        P("sec", None),
    )
    return jax.shard_map(
        per_device,
        mesh=mesh,
        in_specs=placed,
        out_specs=(
            P(("sec", "rad"), None),
            P(None, ("sec", "rad"), None),
            P("sec", "rad", None, None),
        ),
        check_vma=False,
    )
```
